512 devices in a mesh: dp: 32 (over y, x), col: 16 (over z, core).
Axes of the slice: x: 4, y: 8, z: 8, core: 2. Of those that a mesh axis runs over, the one named last changes fastest.
Arguments:
- source_feats: bfloat16 [768, 131072], P('col', 'dp'), may hold values from -6 to 6
- neighbours: int32 [65536, 25], P('dp'), may hold values from 0 to 4095
- degree: int32 [65536], P('dp'), may hold values from 0 to 25
- counts: int32 [32], P('dp'), may hold values from 256 to 2048, as said below
- upstream: bfloat16 [65536, 1024], P(('dp', 'col')), may hold values from -6 to 6
- preact: bfloat16 [65536, 1024], P(('dp', 'col')), may hold values from -6 to 6
Outputs:
- grad_self: float32 [768, 1024], P('col')
- grad_neigh: float32 [768, 1024], P('col')
- grad_bias: float32 [1024], replicated
The draws below stay inside these ranges and needn't reach their ends.
Inputs may be any that keep to these rules, and one draw needn't show every extreme that they name: `neighbours`: each dp block's neighbour indices point into that block's 4096 sources. `counts`: some dp index owns all 2048 slots in every draw.
All inputs are finite; a program needn't handle non-finite values.
Results may differ from the reference program's by a relative error of at most 0.0026.
Values may be sent and summed in bfloat16 or wider, within the bound.
A program may use at most 64 MiB of HBM per device.

```python
import jax
import jax.numpy as jnp
from jax import lax

F = 768
H = 1024
K = 25
T_DEV = 2048
SRC_DEV = 4096
TARGETS = 65536
SOURCES = 131072
N_DP = 32


def draw_degree(key, part):
    key = jax.random.fold_in(key, 11)
    return jax.random.randint(key, (TARGETS,), 0, K + 1).astype(jnp.int32)


def draw_counts(key, part):
    key = jax.random.fold_in(key, 23)
    first, second = jax.random.split(key)
    spread = jax.random.randint(first, (N_DP,), 0, 1024).astype(jnp.int32)
    base = T_DEV // 8
    counts = base + (T_DEV - base) * spread // 1024 * spread // 1024
    chosen = jax.random.randint(second, (), 0, N_DP)
    return jnp.where(jnp.arange(N_DP) == chosen, T_DEV, counts).astype(jnp.int32)


def with_ends(values, stream_key, low, largest):
    spot = [jax.random.randint(jax.random.fold_in(stream_key, axis), (), 0, length) for axis, length in enumerate(values.shape)]
    widest = values.shape.index(max(values.shape))
    neighbour = spot[:widest] + [(spot[widest] + 1) % values.shape[widest]] + spot[widest + 1:]
    return values.at[tuple(spot)].set(low).at[tuple(neighbour)].set(largest)


def levels(rng, extent, cuts, smallest, high):
    def one(axis_at, shards_of):
        steps = jax.random.uniform(jax.random.fold_in(jax.random.fold_in(rng, 6), axis_at), (shards_of,), jnp.float32, smallest / len(cuts), high / len(cuts))
        return jnp.repeat(jnp.exp(steps), extent[axis_at] // shards_of).reshape((-1,) + (1,) * (len(extent) - axis_at - 1))

    factor_of = one(*cuts[0])
    for cut in cuts[1:]:
        factor_of = factor_of * one(*cut)
    return factor_of


def noise(key, shape, scale, limit, cuts=(), kind=jnp.bfloat16):
    values = jax.random.normal(key, shape, jnp.float32) * scale
    if len(cuts) > 0:
        values = levels(key, shape, cuts, -0.22, 0.18) * values
    return jnp.clip(values, min=-limit, max=limit).astype(kind)


def setup_inputs(seed: int = 0) -> dict:
    splits = jax.random.split(jax.random.key(seed), 7)
    source_feats = noise(splits[0], (F, SOURCES), 1.0, 6.0, ((0, 16), (1, 32)))
    neighbours = with_ends(jax.random.randint(splits[1], (TARGETS, K), 0, SRC_DEV), jax.random.fold_in(splits[1], 1), 0, SRC_DEV - 1).astype(jnp.int32)
    degree = draw_degree(jax.random.fold_in(splits[6], 71), 0)
    counts = draw_counts(jax.random.fold_in(splits[6], 71), 0)
    upstream = noise(splits[4], (TARGETS, H), 1.0, 6.0, ((0, 512),))
    preact = noise(splits[5], (TARGETS, H), 1.0, 6.0, ((0, 512),))
    return dict(source_feats=source_feats, neighbours=neighbours, degree=degree, counts=counts, upstream=upstream, preact=preact)


def reference(source_feats, neighbours, degree, counts, upstream, preact):
    slot = jnp.arange(TARGETS, dtype=jnp.int32)
    owner = slot // T_DEV
    live = slot - owner * T_DEV < counts[owner]
    dz = jnp.where((preact > 0) & live[:, None], upstream, jnp.zeros_like(upstream)).astype(jnp.bfloat16)

    def one_block(block_id):
        feats = lax.dynamic_slice_in_dim(source_feats, block_id * SRC_DEV, SRC_DEV, 1)
        index = lax.dynamic_slice_in_dim(neighbours, block_id * T_DEV, T_DEV, 0)
        deg = lax.dynamic_slice_in_dim(degree, block_id * T_DEV, T_DEV, 0)
        total = jnp.zeros((F, T_DEV), jnp.float32)
        for k in range(K):
            picked = jnp.take(feats, index[:, k], axis=1).astype(jnp.float32)
            total = total + jnp.where((deg > k)[None, :], picked, jnp.float32(0.0))
        agg = (total / jnp.maximum(deg, 1).astype(jnp.float32)[None, :]).astype(jnp.bfloat16)
        return (feats[:, :T_DEV], agg)
    selfs, aggs = lax.map(one_block, jnp.arange(N_DP, dtype=jnp.int32))
    self_feats = jnp.transpose(selfs, (1, 0, 2)).reshape(F, TARGETS)
    agg = jnp.transpose(aggs, (1, 0, 2)).reshape(F, TARGETS)
    scale = jnp.float32(1.0) / jnp.sqrt(jnp.float32(TARGETS))
    grad_self = jnp.dot(self_feats, dz, preferred_element_type=jnp.float32) * scale
    grad_neigh = jnp.dot(agg, dz, preferred_element_type=jnp.float32) * scale
    grad_bias = lax.optimization_barrier(jnp.sum(dz.astype(jnp.float32), axis=0)) * scale
    return (grad_self, grad_neigh, grad_bias)
```

```python
import jax
import jax.numpy as jnp
from jax import lax
from jax.experimental import pallas as pl
from jax.experimental.pallas import tpu as pltpu
from jax.sharding import PartitionSpec as P

MESH = pl.DeviceIdType.MESH
NT = (((1,), (1,)), ((), ()))
NZ, NY, NX = 8, 8, 4
NDP, NCOL = NY * NX, NZ * 2
C = 2
H = 1024
W = H // C
ROWS = 128
T = 2048
F = 48
NP = NDP - 1


def encode(nbr_ref, deg_ref, hi_s, lo_s):
    k, t = nbr_ref.shape
    nb = nbr_ref[...]
    live = lax.broadcasted_iota(jnp.int32, (k, t), 0) < deg_ref[...]
    j = lax.broadcasted_iota(jnp.int32, (k, t), 1) // 256
    hi = jnp.where(live, (nb >> 8) * 8 + j, 255).astype(jnp.float32)
    lo = (nb & 255).astype(jnp.float32)
    pad = jnp.full((32 - k, t), 255.0, jnp.float32)
    for code, out in ((hi, hi_s), (lo, lo_s)):
        code = jnp.concatenate([code, pad], axis=0)
        out[...] = jnp.concatenate([code[:, i * 256 : (i + 1) * 256] for i in range(8)], axis=0).T


def tally(hi_s, lo_s, g, rows_hi, rows_lo):
    one, zero = jnp.ones((), jnp.bfloat16), jnp.zeros((), jnp.bfloat16)
    h = jnp.broadcast_to(hi_s[pl.ds(g, 1), :], (16, 256)).astype(jnp.bfloat16)
    l = jnp.broadcast_to(lo_s[pl.ds(g, 1), :], (16, 256)).astype(jnp.bfloat16)
    left = jnp.where(rows_hi == h[None], one, zero).reshape(128, 256)
    right = jnp.where(rows_lo == l[None], one, zero).reshape(256, 256)
    return lax.dot_general(left, right, NT, preferred_element_type=jnp.float32)


def aggregate_block(b, src_s, hi_s, lo_s, tal, agg_s):
    def rows(n):
        ids = lax.broadcasted_iota(jnp.int32, (n, 256), 0).astype(jnp.float32)
        return ids.astype(jnp.bfloat16).reshape(n // 16, 16, 256)

    rows_hi, rows_lo = rows(128), rows(256)

    def pair(p, _):
        g = b * 32 + p * 2
        first = tally(hi_s, lo_s, g, rows_hi, rows_lo).reshape(16, 1, 8, 256)
        second = tally(hi_s, lo_s, g + 1, rows_hi, rows_lo).reshape(16, 1, 8, 256)
        both = jnp.concatenate([first, second], axis=1).reshape(16, 16, 256)
        tal[:, pl.ds(pl.multiple_of(p * 16, 16), 16), :] = both.astype(jnp.bfloat16)
        return 0

    lax.fori_loop(0, 16, pair, 0, unroll=8)
    total = jnp.zeros((256, F), jnp.float32)
    for h in range(16):
        total += lax.dot_general(tal[h], src_s[:, h * 256 : (h + 1) * 256], NT, preferred_element_type=jnp.float32)
    agg_s[pl.ds(pl.multiple_of(b * 256, 256), 256), 0:F] = total


def kernel(
    src_hbm, nbr_hbm, deg_hbm, counts_ref, up_hbm, pre_hbm,
    self_ref, neigh_ref, bias_ref,
    src_s, nbr_s, deg_s, up_s, pre_s, hi_s, lo_s, tal, agg_s, lhs, dz, part, rs, mine, ag,
    load_sem, up_send, up_recv, dn_send, dn_recv, sib_send, sib_recv, rs_send, rs_recv, ag_send, ag_recv,
):
    dp, col = lax.axis_index("dp"), lax.axis_index("col")
    y, x, z, core = dp // NX, dp % NX, col // 2, col % 2
    above, below = (z + 1) % NZ * 2 + core, (z + NZ - 1) % NZ * 2 + core
    sibling = z * 2 + 1 - core

    def peer(d):
        return (y + d // NX) % NY * NX + (x + d % NX) % NX

    barrier = pltpu.get_barrier_semaphore()
    for near in (above, below, sibling):
        pl.semaphore_signal(barrier, inc=1, device_id=(dp, near), device_id_type=MESH)

    loads = [
        pltpu.make_async_copy(a, b, load_sem.at[i])
        for i, (a, b) in enumerate(
            ((up_hbm, up_s), (pre_hbm, pre_s), (nbr_hbm, nbr_s), (deg_hbm, deg_s), (src_hbm, src_s))
        )
    ]
    for load in loads:
        load.start()

    def greet(d, _):
        pl.semaphore_signal(barrier, inc=1, device_id=(peer(d), col), device_id_type=MESH)
        return 0

    lax.fori_loop(1, NDP, greet, 0)

    loads[0].wait()
    loads[1].wait()
    limit = counts_ref[0]
    row = col * ROWS + lax.broadcasted_iota(jnp.int32, (ROWS, W), 0)
    for q in range(C):
        at = slice(q * W, (q + 1) * W)
        keep = (pre_s[:, at].astype(jnp.float32) > 0) & (row < limit)
        dz[q, col] = jnp.where(keep, up_s[:, at].astype(jnp.float32), 0.0).astype(jnp.bfloat16)

    pl.semaphore_wait(barrier, 3 + NP)

    def send(ref, send_sem, recv_sem, to):
        return pltpu.make_async_remote_copy(
            src_ref=ref, dst_ref=ref, send_sem=send_sem, recv_sem=recv_sem, device_id=to, device_id_type=MESH
        )

    def up(q, s, slot, rows):
        return send(dz.at[q, slot, rows], up_send.at[q, s], up_recv.at[q, s], (dp, above))

    def dn(q, s, slot, rows):
        return send(dz.at[q, slot, rows], dn_send.at[q, s], dn_recv.at[q, s], (dp, below))

    def sib(q, i, slot):
        return send(dz.at[q, slot], sib_send.at[q, i], sib_recv.at[q, i], (dp, sibling))

    whole, low, high = pl.ds(0, ROWS), pl.ds(0, ROWS // 2), pl.ds(ROWS // 2, ROWS // 2)
    for q in range(C):
        up(q, 0, col, whole).start()
        dn(q, 0, col, whole).start()
        sib(q, 0, col).start()

    def serve(s, q):
        from_below = (z + NZ - s) % NZ * 2 + core
        from_above = (z + s) % NZ * 2 + core

        @pl.when(s < 4)
        def _():
            up(q, s - 1, from_below, whole).wait_recv()

            @pl.when(s < 3)
            def _():
                up(q, s, from_below, whole).start()

            @pl.when(s == 3)
            def _():
                up(q, s, from_below, low).start()

            dn(q, s - 1, from_above, whole).wait_recv()

            @pl.when(s < 3)
            def _():
                dn(q, s, from_above, whole).start()

            @pl.when(s == 3)
            def _():
                dn(q, s, from_above, high).start()

            sib(q, s, from_below).start()
            sib(q, 3 + s, from_above).start()

        @pl.when(s == 4)
        def _():
            up(q, s - 1, from_below, low).wait_recv()
            dn(q, s - 1, from_below, high).wait_recv()
            sib(q, 7, from_below).start()

    loads[2].wait()
    loads[3].wait()
    encode(nbr_s, deg_s, hi_s, lo_s)
    loads[4].wait()

    def step(i, _):
        aggregate_block(i, src_s, hi_s, lo_s, tal, agg_s)
        serve(1 + i // C, i % C)
        return 0

    lax.fori_loop(0, 8, step, 0)

    lhs[0:F] = src_s[:, 0:T]
    for j in range(8):
        at = slice(j * 256, (j + 1) * 256)
        total = agg_s[pl.ds(j, 256, stride=8), :].T
        lhs[F : 2 * F, at] = (total[0:F] / jnp.maximum(deg_s[:, at], 1).astype(jnp.float32)).astype(jnp.bfloat16)
    lhs[2 * F : 2 * F + 16] = jnp.ones((16, T), jnp.bfloat16)

    scale = jnp.float32(1.0) / jnp.sqrt(jnp.float32(T * NDP))
    for q in range(C):
        for i in range(8):
            slot = lax.rem(z + NZ, NZ) * 2 + core
            sib(q, i, slot).wait_recv()
        grad = jnp.dot(lhs[...], dz[q].reshape(T, W), preferred_element_type=jnp.float32)
        for b in range(W // 128):
            at = slice(b * 128, (b + 1) * 128)
            for a in range(4):
                part[a * 8 + q * (W // 128) + b, 0:24] = grad[a * 24 : a * 24 + 24, at]
                part[a * 8 + q * (W // 128) + b, 24:32] = grad[96:104, at]

    def rs_copy(d):
        return pltpu.make_async_remote_copy(
            src_ref=part.at[peer(d)], dst_ref=rs.at[d], send_sem=rs_send, recv_sem=rs_recv,
            device_id=(peer(d), col), device_id_type=MESH,
        )

    def rs_start(d, _):
        rs_copy(d).start()
        return 0

    lax.fori_loop(1, NDP, rs_start, 0)
    rs[0] = part[dp]
    pltpu.make_async_copy(rs.at[pl.ds(1, NP)], rs.at[pl.ds(1, NP)], rs_recv).wait()

    total = rs[0]
    for d in range(1, NDP):
        total += rs[d]
    mine[...] = total * scale
    ag[dp] = mine[...]

    def ag_start(d, _):
        pltpu.make_async_remote_copy(
            src_ref=mine, dst_ref=ag.at[dp], send_sem=ag_send, recv_sem=ag_recv,
            device_id=(peer(d), col), device_id_type=MESH,
        ).start()
        return 0

    lax.fori_loop(1, NDP, ag_start, 0)
    pltpu.make_async_copy(ag.at[pl.ds(1, NP)], ag.at[pl.ds(1, NP)], ag_recv).wait()
    for b in range(8):
        at = slice(b * 128, (b + 1) * 128)
        for a in range(2):
            self_ref[a * 24 : a * 24 + 24, at] = ag[a * 8 + b, 0:24]
            neigh_ref[a * 24 : a * 24 + 24, at] = ag[(a + 2) * 8 + b, 0:24]
        bias_ref[:, at] = ag[b, 24:25]

    for q in range(C):
        for s in range(4):
            up(q, s, col, whole if s < 3 else low).wait_send()
            dn(q, s, col, whole if s < 3 else high).wait_send()
        for i in range(8):
            sib(q, i, col).wait_send()
    pltpu.make_async_copy(part.at[pl.ds(1, NP)], part.at[pl.ds(1, NP)], rs_send).wait()
    pltpu.make_async_copy(ag.at[pl.ds(1, NP)], ag.at[pl.ds(1, NP)], ag_send).wait()


def per_device(source_feats, neighbours, degree, counts, upstream, preact):
    any_, vmem = pl.BlockSpec(memory_space=pl.ANY), pl.BlockSpec(memory_space=pltpu.VMEM)
    dma = pltpu.SemaphoreType.DMA
    f32, bf16, i32 = jnp.float32, jnp.bfloat16, jnp.int32
    grad = jax.ShapeDtypeStruct((F, H), f32)
    out = pl.pallas_call(
        kernel,
        out_shape=(grad, grad, jax.ShapeDtypeStruct((1, H), f32)),
        in_specs=[any_, any_, any_, pl.BlockSpec(memory_space=pltpu.SMEM), any_, any_],
        out_specs=(vmem, vmem, vmem),
        scratch_shapes=[
            pltpu.VMEM((F, 4096), bf16),
            pltpu.VMEM((25, T), i32),
            pltpu.VMEM((1, T), i32),
            pltpu.VMEM((ROWS, H), bf16),
            pltpu.VMEM((ROWS, H), bf16),
            pltpu.VMEM((256, 256), f32),
            pltpu.VMEM((256, 256), f32),
            pltpu.VMEM((16, 256, 256), bf16),
            pltpu.VMEM((T, 128), f32),
            pltpu.VMEM((2 * F + 16, T), bf16),
            pltpu.VMEM((C, NCOL, ROWS, W), bf16),
            pltpu.VMEM((NDP, 32, 128), f32),
            pltpu.VMEM((NDP, 32, 128), f32),
            pltpu.VMEM((32, 128), f32),
            pltpu.VMEM((NDP, 32, 128), f32),
            dma((5,)),
            dma((C, 4)), dma((C, 4)), dma((C, 4)), dma((C, 4)), dma((C, 8)), dma((C, 8)),
            dma(()), dma(()), dma(()), dma(()),
        ],
        compiler_params=pltpu.CompilerParams(collective_id=0, has_side_effects=True, vmem_limit_bytes=40 << 20),
        name="sage_grads",
    )(source_feats, neighbours.T, degree.reshape(1, T), counts, upstream, preact)
    return out[0], out[1], out[2].reshape(H)


def solution(mesh):
    placed = (P("col", "dp"), P("dp", None), P("dp"), P("dp"), P(("dp", "col"), None), P(("dp", "col"), None))
    return jax.shard_map(
        per_device,
        mesh=mesh,
        in_specs=placed,
        out_specs=(P("col", None), P("col", None), P()),
        check_vma=False,
    )
```

```python
import jax
import jax.numpy as jnp
from jax import lax
from jax.experimental import pallas as pl
from jax.experimental.pallas import tpu as pltpu
from jax.sharding import PartitionSpec as P

MESH = pl.DeviceIdType.MESH
NT = (((1,), (1,)), ((), ()))
NZ, NY, NX = 8, 8, 4
NDP, NCOL = NY * NX, NZ * 2
C = 2
H = 1024
W = H // C
ROWS = 128
T = 2048
F = 48
NP = NDP - 1
ONEHOT = jnp.float8_e4m3fn
PEERS = sorted(
    ((dy, dx) for dy in range(NY) for dx in range(NX) if dy or dx),
    key=lambda p: -(min(p[0], NY - p[0]) + min(p[1], NX - p[1])),
)


def encode(nbr_ref, deg_ref, hi_s, lo_s):
    k, t = nbr_ref.shape
    nb = nbr_ref[...]
    live = lax.broadcasted_iota(jnp.int32, (k, t), 0) < deg_ref[...]
    j = lax.broadcasted_iota(jnp.int32, (k, t), 1) // 256
    hi = jnp.where(live, (nb >> 8) * 8 + j, 255).astype(jnp.float32)
    lo = (nb & 255).astype(jnp.float32)
    pad = jnp.full((32 - k, t), 255.0, jnp.float32)
    for code, out in ((hi, hi_s), (lo, lo_s)):
        code = jnp.concatenate([code, pad], axis=0)
        out[...] = jnp.concatenate([code[:, i * 256 : (i + 1) * 256] for i in range(8)], axis=0).T


def tally(hi_s, lo_s, g, rows_hi, rows_lo):
    one, zero = jnp.ones((), jnp.bfloat16), jnp.zeros((), jnp.bfloat16)
    h = jnp.broadcast_to(hi_s[pl.ds(g, 1), :], (16, 256)).astype(jnp.bfloat16)
    l = jnp.broadcast_to(lo_s[pl.ds(g, 1), :], (16, 256)).astype(jnp.bfloat16)
    left = jnp.where(rows_hi == h[None], one, zero).reshape(128, 256).astype(ONEHOT)
    right = jnp.where(rows_lo == l[None], one, zero).reshape(256, 256).astype(ONEHOT)
    return lax.dot_general(left, right, NT, preferred_element_type=jnp.float32)


def aggregate_block(b, src_s, hi_s, lo_s, tal, agg_s):
    def rows(n):
        ids = lax.broadcasted_iota(jnp.int32, (n, 256), 0).astype(jnp.float32)
        return ids.astype(jnp.bfloat16).reshape(n // 16, 16, 256)

    rows_hi, rows_lo = rows(128), rows(256)

    def pair(p, _):
        g = b * 32 + p * 2
        first = tally(hi_s, lo_s, g, rows_hi, rows_lo).reshape(16, 1, 8, 256)
        second = tally(hi_s, lo_s, g + 1, rows_hi, rows_lo).reshape(16, 1, 8, 256)
        both = jnp.concatenate([first, second], axis=1).reshape(16, 16, 256)
        tal[:, pl.ds(pl.multiple_of(p * 16, 16), 16), :] = both.astype(jnp.bfloat16)
        return 0

    lax.fori_loop(0, 16, pair, 0, unroll=16)
    total = jnp.zeros((256, F), jnp.float32)
    for h in range(16):
        total += lax.dot_general(tal[h], src_s[:, h * 256 : (h + 1) * 256], NT, preferred_element_type=jnp.float32)
    agg_s[pl.ds(pl.multiple_of(b * 256, 256), 256), 0:F] = total


def kernel(
    src_hbm, nbr_hbm, deg_hbm, counts_ref, up_hbm, pre_hbm,
    grad_ref, bias_ref,
    src_s, nbr_s, deg_s, up_s, pre_s, hi_s, lo_s, tal, agg_s, lhs, dz, acc, part, rs, mine,
    load_sem, up_send, up_recv, dn_send, dn_recv, sib_send, sib_recv, rs_send, rs_recv, ag_send, ag_recv, own_sem,
):
    dp, col = lax.axis_index("dp"), lax.axis_index("col")
    y, x, z, core = dp // NX, dp % NX, col // 2, col % 2
    above, below = (z + 1) % NZ * 2 + core, (z + NZ - 1) % NZ * 2 + core
    sibling = z * 2 + 1 - core

    def peer(dy, dx):
        return (y + dy) % NY * NX + (x + dx) % NX

    barrier = pltpu.get_barrier_semaphore()
    for near in (above, below, sibling):
        pl.semaphore_signal(barrier, inc=1, device_id=(dp, near), device_id_type=MESH)

    loads = [
        pltpu.make_async_copy(a, b, load_sem.at[i])
        for i, (a, b) in enumerate(
            ((up_hbm, up_s), (pre_hbm, pre_s), (nbr_hbm, nbr_s), (deg_hbm, deg_s), (src_hbm, src_s))
        )
    ]
    for load in loads:
        load.start()

    for p in PEERS:
        pl.semaphore_signal(barrier, inc=1, device_id=(peer(*p), col), device_id_type=MESH)

    loads[0].wait()
    loads[1].wait()
    limit = counts_ref[0]
    row = col * ROWS + lax.broadcasted_iota(jnp.int32, (ROWS, W), 0)
    for q in range(C):
        at = slice(q * W, (q + 1) * W)
        keep = (pre_s[:, at].astype(jnp.float32) > 0) & (row < limit)
        dz[q, col] = jnp.where(keep, up_s[:, at].astype(jnp.float32), 0.0).astype(jnp.bfloat16)

    pl.semaphore_wait(barrier, 3 + NP)

    def send(ref, send_sem, recv_sem, to):
        return pltpu.make_async_remote_copy(
            src_ref=ref, dst_ref=ref, send_sem=send_sem, recv_sem=recv_sem, device_id=to, device_id_type=MESH
        )

    def up(q, s, slot, rows):
        return send(dz.at[q, slot, rows], up_send.at[q, s], up_recv.at[q, s], (dp, above))

    def dn(q, s, slot, rows):
        return send(dz.at[q, slot, rows], dn_send.at[q, s], dn_recv.at[q, s], (dp, below))

    def sib(q, i, slot):
        return send(dz.at[q, slot], sib_send.at[q, i], sib_recv.at[q, i], (dp, sibling))

    whole, low, high = pl.ds(0, ROWS), pl.ds(0, ROWS // 2), pl.ds(ROWS // 2, ROWS // 2)
    for q in range(C):
        up(q, 0, col, whole).start()
        dn(q, 0, col, whole).start()
        sib(q, 0, col).start()

    def serve(s, q):
        from_below = (z + NZ - s) % NZ * 2 + core
        from_above = (z + s) % NZ * 2 + core
        if s == 4:
            up(q, s - 1, from_below, low).wait_recv()
            dn(q, s - 1, from_below, high).wait_recv()
            sib(q, 7, from_below).start()
            return
        up(q, s - 1, from_below, whole).wait_recv()
        up(q, s, from_below, whole if s < 3 else low).start()
        dn(q, s - 1, from_above, whole).wait_recv()
        dn(q, s, from_above, whole if s < 3 else high).start()
        sib(q, s, from_below).start()
        sib(q, 3 + s, from_above).start()

    def add(dz_, i):
        at = (z + NZ + dz_) % NZ
        for q in range(C):
            sib(q, i, at * 2 + 1 - core).wait_recv()
        rows = lhs[:, pl.ds(pl.multiple_of(at * 2 * ROWS, 2 * ROWS), 2 * ROWS)]
        for q in range(C):
            new = jnp.dot(rows, dz[q, pl.ds(at * 2, 2)].reshape(2 * ROWS, W), preferred_element_type=jnp.float32)
            here = slice(q * W, (q + 1) * W)
            acc[:, here] = new if dz_ == 0 else acc[:, here] + new

    loads[2].wait()
    loads[3].wait()
    encode(nbr_s, deg_s, hi_s, lo_s)
    loads[4].wait()

    def step(i, _):
        aggregate_block(i, src_s, hi_s, lo_s, tal, agg_s)
        for at, turn in ((3, (1, 0)), (4, (1, 1)), (7, (2, 0))):
            pl.when(i == at)(lambda turn=turn: serve(*turn))
        return 0

    lax.fori_loop(0, 8, step, 0)

    lhs[0:F] = src_s[:, 0:T]
    for j in range(8):
        at = slice(j * 256, (j + 1) * 256)
        total = agg_s[pl.ds(j, 256, stride=8), :].T
        lhs[F : 2 * F, at] = (total[0:F] / jnp.maximum(deg_s[:, at], 1).astype(jnp.float32)).astype(jnp.bfloat16)
    lhs[2 * F : 2 * F + 16] = jnp.ones((16, T), jnp.bfloat16)

    serve(2, 1)
    add(0, 0)
    add(-1, 1)
    add(1, 4)
    serve(3, 0)
    serve(3, 1)
    add(-2, 2)
    add(2, 5)
    serve(4, 0)
    serve(4, 1)
    add(-3, 3)
    add(3, 6)
    add(4, 7)

    bias = jnp.concatenate([acc[2 * F : 2 * F + 1, b * 128 : (b + 1) * 128] for b in range(8)], axis=0)
    for a in range(4):
        for b in range(8):
            rows = acc[a * 24 : a * 24 + 24, b * 128 : (b + 1) * 128]
            part[a * 8 + b] = jnp.concatenate([rows, bias], axis=0).astype(jnp.bfloat16)

    for p in PEERS:
        pltpu.make_async_remote_copy(
            src_ref=part.at[peer(*p)], dst_ref=rs.at[dp], send_sem=rs_send, recv_sem=rs_recv,
            device_id=(peer(*p), col), device_id_type=MESH,
        ).start()
    rs[dp] = part[dp]
    pltpu.make_async_copy(rs.at[pl.ds(0, NP)], rs.at[pl.ds(0, NP)], rs_recv).wait()

    scale = jnp.float32(1.0) / jnp.sqrt(jnp.float32(T * NDP))
    total = rs[0].astype(jnp.float32)
    for d in range(1, NDP):
        total += rs[d].astype(jnp.float32)
    total *= scale
    mine[...] = total[0:24]
    bias_ref[...] = total[24:32]

    rows, cols = pl.ds(pl.multiple_of(dp // 8 * 24, 8), 24), pl.ds(pl.multiple_of(dp % 8 * 128, 128), 128)
    for p in PEERS:
        pltpu.make_async_remote_copy(
            src_ref=mine, dst_ref=grad_ref.at[rows, cols], send_sem=ag_send, recv_sem=ag_recv,
            device_id=(peer(*p), col), device_id_type=MESH,
        ).start()
    own = pltpu.make_async_copy(mine, grad_ref.at[rows, cols], own_sem)
    own.start()

    for q in range(C):
        for s in range(4):
            up(q, s, col, whole if s < 3 else low).wait_send()
            dn(q, s, col, whole if s < 3 else high).wait_send()
        for i in range(8):
            sib(q, i, col).wait_send()
    pltpu.make_async_copy(part.at[pl.ds(0, NP)], part.at[pl.ds(0, NP)], rs_send).wait()
    own.wait()
    every = agg_s.at[pl.ds(0, NP * 24)]
    pltpu.make_async_copy(every, every, ag_send).wait()
    pltpu.make_async_copy(every, every, ag_recv).wait()


def place(grad_ref, bias_ref, self_ref, neigh_ref, out_ref, sems):
    copies = (
        pltpu.make_async_copy(grad_ref.at[pl.ds(0, F)], self_ref, sems.at[0]),
        pltpu.make_async_copy(grad_ref.at[pl.ds(F, F)], neigh_ref, sems.at[1]),
        pltpu.make_async_copy(bias_ref, out_ref, sems.at[2]),
    )
    for copy in copies:
        copy.start()
    for copy in copies:
        copy.wait()


def per_device(source_feats, neighbours, degree, counts, upstream, preact):
    any_, vmem = pl.BlockSpec(memory_space=pl.ANY), pl.BlockSpec(memory_space=pltpu.VMEM)
    dma = pltpu.SemaphoreType.DMA
    f32, bf16, i32 = jnp.float32, jnp.bfloat16, jnp.int32
    grad, bias = pl.pallas_call(
        kernel,
        out_shape=(jax.ShapeDtypeStruct((2 * F, H), f32), jax.ShapeDtypeStruct((8, 128), f32)),
        in_specs=[any_, any_, any_, pl.BlockSpec(memory_space=pltpu.SMEM), any_, any_],
        out_specs=(any_, vmem),
        scratch_shapes=[
            pltpu.VMEM((F, 4096), bf16),
            pltpu.VMEM((25, T), i32),
            pltpu.VMEM((1, T), i32),
            pltpu.VMEM((ROWS, H), bf16),
            pltpu.VMEM((ROWS, H), bf16),
            pltpu.VMEM((256, 256), f32),
            pltpu.VMEM((256, 256), f32),
            pltpu.VMEM((16, 256, 256), bf16),
            pltpu.VMEM((T, 128), f32),
            pltpu.VMEM((2 * F + 16, T), bf16),
            pltpu.VMEM((C, NCOL, ROWS, W), bf16),
            pltpu.VMEM((2 * F + 16, H), f32),
            pltpu.VMEM((NDP, 32, 128), bf16),
            pltpu.VMEM((NDP, 32, 128), bf16),
            pltpu.VMEM((24, 128), f32),
            dma((5,)),
            dma((C, 4)), dma((C, 4)), dma((C, 4)), dma((C, 4)), dma((C, 8)), dma((C, 8)),
            dma(()), dma(()), dma(()), dma(()), dma(()),
        ],
        compiler_params=pltpu.CompilerParams(collective_id=0, has_side_effects=True, vmem_limit_bytes=60 << 20),
        name="sage_grads",
    )(source_feats, neighbours.T, degree.reshape(1, T), counts, upstream, preact)
    own, neigh, bias = pl.pallas_call(
        place,
        out_shape=(jax.ShapeDtypeStruct((F, H), f32), jax.ShapeDtypeStruct((F, H), f32), jax.ShapeDtypeStruct((8, 128), f32)),
        in_specs=[any_, any_],
        out_specs=(any_, any_, any_),
        scratch_shapes=[dma((3,))],
        compiler_params=pltpu.CompilerParams(vmem_limit_bytes=60 << 20),
        name="place",
    )(grad, bias)
    return own, neigh, bias.reshape(H)


def solution(mesh):
    placed = (P("col", "dp"), P("dp", None), P("dp"), P("dp"), P(("dp", "col"), None), P(("dp", "col"), None))
    return jax.shard_map(
        per_device,
        mesh=mesh,
        in_specs=placed,
        out_specs=(P("col", None), P("col", None), P()),
        check_vma=False,
    )
```

```python
import jax
import jax.numpy as jnp
from jax import lax
from jax.experimental import pallas as pl
from jax.experimental.pallas import tpu as pltpu
from jax.sharding import PartitionSpec as P

MESH = pl.DeviceIdType.MESH
NT = (((1,), (1,)), ((), ()))
NZ, NY, NX = 8, 8, 4
NDP, NCOL = NY * NX, NZ * 2
C = 2
H = 1024
W = H // C
ROWS = 128
T = 2048
F = 48
NP = NDP - 1
ONEHOT = jnp.float8_e4m3fn
PEERS = sorted(
    ((dy, dx) for dy in range(NY) for dx in range(NX) if dy or dx),
    key=lambda p: -(min(p[0], NY - p[0]) + min(p[1], NX - p[1])),
)


def encode(nbr_ref, deg_ref, hi_s, lo_s):
    k, t = nbr_ref.shape
    nb = nbr_ref[...]
    live = lax.broadcasted_iota(jnp.int32, (k, t), 0) < deg_ref[...]
    j = lax.broadcasted_iota(jnp.int32, (k, t), 1) // 256
    hi = jnp.where(live, (nb >> 8) * 8 + j, 255).astype(jnp.float32)
    lo = (nb & 255).astype(jnp.float32)
    pad = jnp.full((32 - k, t), 255.0, jnp.float32)
    for code, out in ((hi, hi_s), (lo, lo_s)):
        code = jnp.concatenate([code, pad], axis=0)
        out[...] = jnp.concatenate([code[:, i * 256 : (i + 1) * 256] for i in range(8)], axis=0).T


def tally(hi_s, lo_s, g, rows_hi, rows_lo):
    one, zero = jnp.ones((), jnp.bfloat16), jnp.zeros((), jnp.bfloat16)
    h = jnp.broadcast_to(hi_s[pl.ds(g, 1), :], (16, 256)).astype(jnp.bfloat16)
    l = jnp.broadcast_to(lo_s[pl.ds(g, 1), :], (16, 256)).astype(jnp.bfloat16)
    left = jnp.where(rows_hi == h[None], one, zero).reshape(128, 256).astype(ONEHOT)
    right = jnp.where(rows_lo == l[None], one, zero).reshape(256, 256).astype(ONEHOT)
    return lax.dot_general(left, right, NT, preferred_element_type=jnp.float32)


def aggregate_block(b, src_s, hi_s, lo_s, tal, agg_s):
    def rows(n):
        ids = lax.broadcasted_iota(jnp.int32, (n, 256), 0).astype(jnp.float32)
        return ids.astype(jnp.bfloat16).reshape(n // 16, 16, 256)

    rows_hi, rows_lo = rows(128), rows(256)

    def pair(p, _):
        g = b * 32 + p * 2
        first = tally(hi_s, lo_s, g, rows_hi, rows_lo).reshape(16, 1, 8, 256)
        second = tally(hi_s, lo_s, g + 1, rows_hi, rows_lo).reshape(16, 1, 8, 256)
        both = jnp.concatenate([first, second], axis=1).reshape(16, 16, 256)
        tal[:, pl.ds(pl.multiple_of(p * 16, 16), 16), :] = both.astype(jnp.bfloat16)
        return 0

    lax.fori_loop(0, 16, pair, 0, unroll=16)
    total = jnp.zeros((256, F), jnp.float32)
    for h in range(16):
        total += lax.dot_general(tal[h], src_s[:, h * 256 : (h + 1) * 256], NT, preferred_element_type=jnp.float32)
    agg_s[pl.ds(pl.multiple_of(b * 256, 256), 256), 0:F] = total


def kernel(
    src_hbm, nbr_hbm, deg_hbm, counts_ref, up_hbm, pre_hbm,
    grad_ref, bias_ref,
    src_s, nbr_s, deg_s, up_s, pre_s, hi_s, lo_s, tal, agg_s, lhs, dz, acc, part, rs, mine,
    load_sem, up_send, up_recv, dn_send, dn_recv, sib_send, sib_recv, rs_send, rs_recv, ag_send, ag_recv, own_sem, news,
):
    dp, col = lax.axis_index("dp"), lax.axis_index("col")
    y, x, z, core = dp // NX, dp % NX, col // 2, col % 2
    above, below = (z + 1) % NZ * 2 + core, (z + NZ - 1) % NZ * 2 + core
    sibling = z * 2 + 1 - core

    def peer(dy, dx):
        return (y + dy) % NY * NX + (x + dx) % NX

    barrier = pltpu.get_barrier_semaphore()
    beside_x, beside_y = (peer(0, 1), peer(0, NX - 1)), (peer(1, 0), peer(NY - 1, 0))
    near = [(dp, above), (dp, below), (dp, sibling)] + [(p, col) for p in beside_x + beside_y]
    for to in near:
        pl.semaphore_signal(barrier, inc=1, device_id=to, device_id_type=MESH)

    loads = [
        pltpu.make_async_copy(a, b, load_sem.at[i])
        for i, (a, b) in enumerate(
            ((up_hbm, up_s), (pre_hbm, pre_s), (nbr_hbm, nbr_s), (deg_hbm, deg_s), (src_hbm, src_s))
        )
    ]
    for load in loads:
        load.start()


    loads[0].wait()
    loads[1].wait()
    limit = counts_ref[0]
    row = col * ROWS + lax.broadcasted_iota(jnp.int32, (ROWS, W), 0)
    for q in range(C):
        at = slice(q * W, (q + 1) * W)
        keep = (pre_s[:, at].astype(jnp.float32) > 0) & (row < limit)
        dz[q, col] = jnp.where(keep, up_s[:, at].astype(jnp.float32), 0.0).astype(jnp.bfloat16)

    pl.semaphore_wait(barrier, len(near))

    def tell(n):
        for to in beside_x if n == 0 else beside_y:
            pl.semaphore_signal(news.at[n], inc=1, device_id=(to, col), device_id_type=MESH)

    def hear(n):
        pl.semaphore_wait(news.at[n], 2)
        if n < NY // 2:
            tell(n + 1)

    tell(0)

    def send(ref, send_sem, recv_sem, to):
        return pltpu.make_async_remote_copy(
            src_ref=ref, dst_ref=ref, send_sem=send_sem, recv_sem=recv_sem, device_id=to, device_id_type=MESH
        )

    def up(q, s, slot, rows):
        return send(dz.at[q, slot, rows], up_send.at[q, s], up_recv.at[q, s], (dp, above))

    def dn(q, s, slot, rows):
        return send(dz.at[q, slot, rows], dn_send.at[q, s], dn_recv.at[q, s], (dp, below))

    def sib(q, i, slot):
        return send(dz.at[q, slot], sib_send.at[q, i], sib_recv.at[q, i], (dp, sibling))

    whole, low, high = pl.ds(0, ROWS), pl.ds(0, ROWS // 2), pl.ds(ROWS // 2, ROWS // 2)
    for q in range(C):
        up(q, 0, col, whole).start()
        dn(q, 0, col, whole).start()
        sib(q, 0, col).start()

    def serve(s, q):
        from_below = (z + NZ - s) % NZ * 2 + core
        from_above = (z + s) % NZ * 2 + core
        if s == 4:
            up(q, s - 1, from_below, low).wait_recv()
            dn(q, s - 1, from_below, high).wait_recv()
            sib(q, 7, from_below).start()
            return
        up(q, s - 1, from_below, whole).wait_recv()
        up(q, s, from_below, whole if s < 3 else low).start()
        dn(q, s - 1, from_above, whole).wait_recv()
        dn(q, s, from_above, whole if s < 3 else high).start()
        sib(q, s, from_below).start()
        sib(q, 3 + s, from_above).start()

    def add(dz_, i):
        at = (z + NZ + dz_) % NZ
        for q in range(C):
            sib(q, i, at * 2 + 1 - core).wait_recv()
        rows = lhs[:, pl.ds(pl.multiple_of(at * 2 * ROWS, 2 * ROWS), 2 * ROWS)]
        for q in range(C):
            new = jnp.dot(rows, dz[q, pl.ds(at * 2, 2)].reshape(2 * ROWS, W), preferred_element_type=jnp.float32)
            here = slice(q * W, (q + 1) * W)
            acc[:, here] = new if dz_ == 0 else acc[:, here] + new

    loads[2].wait()
    loads[3].wait()
    encode(nbr_s, deg_s, hi_s, lo_s)
    loads[4].wait()

    def step(i, _):
        aggregate_block(i, src_s, hi_s, lo_s, tal, agg_s)
        for at, n in ((1, 0), (4, 1), (6, 2)):
            pl.when(i == at)(lambda n=n: hear(n))
        for at, turn in ((3, (1, 0)), (4, (1, 1)), (7, (2, 0))):
            pl.when(i == at)(lambda turn=turn: serve(*turn))
        return 0

    lax.fori_loop(0, 8, step, 0)

    lhs[0:F] = src_s[:, 0:T]
    for j in range(8):
        at = slice(j * 256, (j + 1) * 256)
        total = agg_s[pl.ds(j, 256, stride=8), :].T
        lhs[F : 2 * F, at] = (total[0:F] / jnp.maximum(deg_s[:, at], 1).astype(jnp.float32)).astype(jnp.bfloat16)
    lhs[2 * F : 2 * F + 16] = jnp.ones((16, T), jnp.bfloat16)

    serve(2, 1)
    hear(3)
    add(0, 0)
    add(-1, 1)
    add(1, 4)
    serve(3, 0)
    serve(3, 1)
    add(-2, 2)
    add(2, 5)
    serve(4, 0)
    serve(4, 1)
    add(-3, 3)
    add(3, 6)
    add(4, 7)

    bias = jnp.concatenate([acc[2 * F : 2 * F + 1, b * 128 : (b + 1) * 128] for b in range(8)], axis=0)
    for a in range(4):
        for b in range(8):
            rows = acc[a * 24 : a * 24 + 24, b * 128 : (b + 1) * 128]
            part[a * 8 + b] = jnp.concatenate([rows, bias], axis=0).astype(jnp.bfloat16)

    hear(4)
    for p in PEERS:
        pltpu.make_async_remote_copy(
            src_ref=part.at[peer(*p)], dst_ref=rs.at[dp], send_sem=rs_send, recv_sem=rs_recv,
            device_id=(peer(*p), col), device_id_type=MESH,
        ).start()
    rs[dp] = part[dp]
    pltpu.make_async_copy(rs.at[pl.ds(0, NP)], rs.at[pl.ds(0, NP)], rs_recv).wait()

    scale = jnp.float32(1.0) / jnp.sqrt(jnp.float32(T * NDP))
    total = rs[0].astype(jnp.float32)
    for d in range(1, NDP):
        total += rs[d].astype(jnp.float32)
    total *= scale
    mine[...] = total[0:24]
    bias_ref[...] = total[24:32]

    rows, cols = pl.ds(pl.multiple_of(dp // 8 * 24, 8), 24), pl.ds(pl.multiple_of(dp % 8 * 128, 128), 128)
    for p in PEERS:
        pltpu.make_async_remote_copy(
            src_ref=mine, dst_ref=grad_ref.at[rows, cols], send_sem=ag_send, recv_sem=ag_recv,
            device_id=(peer(*p), col), device_id_type=MESH,
        ).start()
    own = pltpu.make_async_copy(mine, grad_ref.at[rows, cols], own_sem)
    own.start()

    for q in range(C):
        for s in range(4):
            up(q, s, col, whole if s < 3 else low).wait_send()
            dn(q, s, col, whole if s < 3 else high).wait_send()
        for i in range(8):
            sib(q, i, col).wait_send()
    pltpu.make_async_copy(part.at[pl.ds(0, NP)], part.at[pl.ds(0, NP)], rs_send).wait()
    own.wait()
    every = agg_s.at[pl.ds(0, NP * 24)]
    pltpu.make_async_copy(every, every, ag_send).wait()
    pltpu.make_async_copy(every, every, ag_recv).wait()


def place(grad_ref, bias_ref, self_ref, neigh_ref, out_ref):
    self_ref[...] = grad_ref[0:F]
    neigh_ref[...] = grad_ref[F : 2 * F]
    out_ref[...] = bias_ref[...]


def per_device(source_feats, neighbours, degree, counts, upstream, preact):
    any_, vmem = pl.BlockSpec(memory_space=pl.ANY), pl.BlockSpec(memory_space=pltpu.VMEM)
    dma = pltpu.SemaphoreType.DMA
    f32, bf16, i32 = jnp.float32, jnp.bfloat16, jnp.int32
    grad, bias = pl.pallas_call(
        kernel,
        out_shape=(jax.ShapeDtypeStruct((2 * F, H), f32), jax.ShapeDtypeStruct((8, 128), f32)),
        in_specs=[any_, any_, any_, pl.BlockSpec(memory_space=pltpu.SMEM), any_, any_],
        out_specs=(any_, vmem),
        scratch_shapes=[
            pltpu.VMEM((F, 4096), bf16),
            pltpu.VMEM((25, T), i32),
            pltpu.VMEM((1, T), i32),
            pltpu.VMEM((ROWS, H), bf16),
            pltpu.VMEM((ROWS, H), bf16),
            pltpu.VMEM((256, 256), f32),
            pltpu.VMEM((256, 256), f32),
            pltpu.VMEM((16, 256, 256), bf16),
            pltpu.VMEM((T, 128), f32),
            pltpu.VMEM((2 * F + 16, T), bf16),
            pltpu.VMEM((C, NCOL, ROWS, W), bf16),
            pltpu.VMEM((2 * F + 16, H), f32),
            pltpu.VMEM((NDP, 32, 128), bf16),
            pltpu.VMEM((NDP, 32, 128), bf16),
            pltpu.VMEM((24, 128), f32),
            dma((5,)),
            dma((C, 4)), dma((C, 4)), dma((C, 4)), dma((C, 4)), dma((C, 8)), dma((C, 8)),
            dma(()), dma(()), dma(()), dma(()), dma(()), pltpu.SemaphoreType.REGULAR((NY // 2 + 1,)),
        ],
        compiler_params=pltpu.CompilerParams(collective_id=0, has_side_effects=True, vmem_limit_bytes=60 << 20),
        name="sage_grads",
    )(source_feats, neighbours.T, degree.reshape(1, T), counts, upstream, preact)
    own, neigh, bias = pl.pallas_call(
        place,
        out_shape=(jax.ShapeDtypeStruct((F, H), f32), jax.ShapeDtypeStruct((F, H), f32), jax.ShapeDtypeStruct((8, 128), f32)),
        in_specs=[vmem, vmem],
        out_specs=(vmem, vmem, vmem),
        compiler_params=pltpu.CompilerParams(vmem_limit_bytes=60 << 20),
        name="place",
    )(grad, bias)
    return own, neigh, bias.reshape(H)


def solution(mesh):
    placed = (P("col", "dp"), P("dp", None), P("dp"), P("dp"), P(("dp", "col"), None), P(("dp", "col"), None))
    return jax.shard_map(
        per_device,
        mesh=mesh,
        in_specs=placed,
        out_specs=(P("col", None), P("col", None), P()),
        check_vma=False,
    )
```

```python
import jax
import jax.numpy as jnp
from jax import lax
from jax.experimental import pallas as pl
from jax.experimental.pallas import tpu as pltpu
from jax.sharding import PartitionSpec as P

MESH = pl.DeviceIdType.MESH
NT = (((1,), (1,)), ((), ()))
NZ, NY, NX = 8, 8, 4
NDP, NCOL = NY * NX, NZ * 2
C = 2
H = 1024
W = H // C
ROWS = 128
T = 2048
F = 48
NP = NDP - 1
ONEHOT = jnp.float8_e4m3fn
PEERS = sorted(
    ((dy, dx) for dy in range(NY) for dx in range(NX) if dy or dx),
    key=lambda p: -(min(p[0], NY - p[0]) + min(p[1], NX - p[1])),
)


def encode(nbr_ref, deg_ref, hi_s, lo_s):
    k, t = nbr_ref.shape
    nb = nbr_ref[...]
    live = lax.broadcasted_iota(jnp.int32, (k, t), 0) < deg_ref[...]
    j = lax.broadcasted_iota(jnp.int32, (k, t), 1) // 256
    hi = jnp.where(live, (nb >> 8) * 8 + j, 255).astype(jnp.float32)
    lo = (nb & 255).astype(jnp.float32)
    pad = jnp.full((32 - k, t), 255.0, jnp.float32)
    for code, out in ((hi, hi_s), (lo, lo_s)):
        code = jnp.concatenate([code, pad], axis=0)
        out[...] = jnp.concatenate([code[:, i * 256 : (i + 1) * 256] for i in range(8)], axis=0).T


def tally(hi_s, lo_s, g, rows_hi, rows_lo):
    one, zero = jnp.ones((), jnp.bfloat16), jnp.zeros((), jnp.bfloat16)
    h = jnp.broadcast_to(hi_s[pl.ds(g, 1), :], (16, 256)).astype(jnp.bfloat16)
    l = jnp.broadcast_to(lo_s[pl.ds(g, 1), :], (16, 256)).astype(jnp.bfloat16)
    left = jnp.where(rows_hi == h[None], one, zero).reshape(128, 256).astype(ONEHOT)
    right = jnp.where(rows_lo == l[None], one, zero).reshape(256, 256).astype(ONEHOT)
    return lax.dot_general(left, right, NT, preferred_element_type=jnp.float32)


def aggregate_block(b, src_s, hi_s, lo_s, tal, agg_s):
    def rows(n):
        ids = lax.broadcasted_iota(jnp.int32, (n, 256), 0).astype(jnp.float32)
        return ids.astype(jnp.bfloat16).reshape(n // 16, 16, 256)

    rows_hi, rows_lo = rows(128), rows(256)

    def pair(p, _):
        g = b * 32 + p * 2
        first = tally(hi_s, lo_s, g, rows_hi, rows_lo).reshape(16, 1, 8, 256)
        second = tally(hi_s, lo_s, g + 1, rows_hi, rows_lo).reshape(16, 1, 8, 256)
        both = jnp.concatenate([first, second], axis=1).reshape(16, 16, 256)
        tal[:, pl.ds(pl.multiple_of(p * 16, 16), 16), :] = both.astype(jnp.bfloat16)
        return 0

    lax.fori_loop(0, 16, pair, 0, unroll=16)
    total = jnp.zeros((256, F), jnp.float32)
    for h in range(16):
        total += lax.dot_general(tal[h], src_s[:, h * 256 : (h + 1) * 256], NT, preferred_element_type=jnp.float32)
    agg_s[pl.ds(pl.multiple_of(b * 256, 256), 256), 0:F] = total


def kernel(
    src_hbm, nbr_hbm, deg_hbm, counts_ref, up_hbm, pre_hbm,
    grad_ref, bias_ref,
    src_s, nbr_s, deg_s, up_s, pre_s, hi_s, lo_s, tal, agg_s, lhs, dz, acc, part, rs, mine,
    load_sem, up_send, up_recv, dn_send, dn_recv, sib_send, sib_recv, rs_send, rs_recv, ag_send, ag_recv, own_sem, news,
):
    dp, col = lax.axis_index("dp"), lax.axis_index("col")
    y, x, z, core = dp // NX, dp % NX, col // 2, col % 2
    above, below = (z + 1) % NZ * 2 + core, (z + NZ - 1) % NZ * 2 + core
    sibling = z * 2 + 1 - core

    def peer(dy, dx):
        return (y + dy) % NY * NX + (x + dx) % NX

    barrier = pltpu.get_barrier_semaphore()
    beside_x, beside_y = (peer(0, 1), peer(0, NX - 1)), (peer(1, 0), peer(NY - 1, 0))
    near = [(dp, above), (dp, below), (dp, sibling)] + [(p, col) for p in beside_x + beside_y]
    for to in near:
        pl.semaphore_signal(barrier, inc=1, device_id=to, device_id_type=MESH)

    loads = [
        pltpu.make_async_copy(a, b, load_sem.at[i])
        for i, (a, b) in enumerate(
            ((up_hbm, up_s), (pre_hbm, pre_s), (nbr_hbm, nbr_s), (deg_hbm, deg_s), (src_hbm, src_s))
        )
    ]
    for load in loads:
        load.start()


    loads[0].wait()
    loads[1].wait()
    limit = counts_ref[0]
    row = col * ROWS + lax.broadcasted_iota(jnp.int32, (ROWS, W), 0)
    for q in range(C):
        at = slice(q * W, (q + 1) * W)
        keep = (pre_s[:, at].astype(jnp.float32) > 0) & (row < limit)
        dz[q, col] = jnp.where(keep, up_s[:, at].astype(jnp.float32), 0.0).astype(jnp.bfloat16)

    pl.semaphore_wait(barrier, len(near))

    def tell(n):
        for to in beside_x if n == 0 else beside_y:
            pl.semaphore_signal(news.at[n], inc=1, device_id=(to, col), device_id_type=MESH)

    def hear(n):
        pl.semaphore_wait(news.at[n], 2)
        if n < NY // 2:
            tell(n + 1)

    tell(0)

    def send(ref, send_sem, recv_sem, to):
        return pltpu.make_async_remote_copy(
            src_ref=ref, dst_ref=ref, send_sem=send_sem, recv_sem=recv_sem, device_id=to, device_id_type=MESH
        )

    halves = pl.ds(0, ROWS // 2), pl.ds(ROWS // 2, ROWS // 2)

    def up(q, s, far, slot):
        n = q * 8 + s * 2 + far
        return send(dz.at[q, slot, halves[1 - far]], up_send.at[n], up_recv.at[n], (dp, above))

    def dn(q, s, far, slot):
        n = q * 8 + s * 2 + far
        return send(dz.at[q, slot, halves[far]], dn_send.at[n], dn_recv.at[n], (dp, below))

    def sib(q, i, slot):
        return send(dz.at[q, slot], sib_send.at[q, i], sib_recv.at[q, i], (dp, sibling))

    for far in (1, 0):
        for q in range(C):
            up(q, 0, far, col).start()
            dn(q, 0, far, col).start()
    for q in range(C):
        sib(q, 0, col).start()

    def serve(q, s, far):
        from_below = (z + NZ - 1 - s) % NZ * 2 + core
        from_above = (z + 1 + s) % NZ * 2 + core
        onward = s < 2 + far
        up(q, s, far, from_below).wait_recv()
        if onward:
            up(q, s + 1, far, from_below).start()
        dn(q, s, far, from_above).wait_recv()
        if onward:
            dn(q, s + 1, far, from_above).start()
        if s == 3:
            sib(q, 7, from_below).start()
        elif not far:
            sib(q, s + 1, from_below).start()
            sib(q, s + 4, from_above).start()

    def add(dz_, i):
        at = (z + NZ + dz_) % NZ
        for q in range(C):
            sib(q, i, at * 2 + 1 - core).wait_recv()
        rows = lhs[:, pl.ds(pl.multiple_of(at * 2 * ROWS, 2 * ROWS), 2 * ROWS)]
        for q in range(C):
            new = jnp.dot(rows, dz[q, pl.ds(at * 2, 2)].reshape(2 * ROWS, W), preferred_element_type=jnp.float32)
            here = slice(q * W, (q + 1) * W)
            acc[:, here] = new if dz_ == 0 else acc[:, here] + new

    loads[2].wait()
    loads[3].wait()
    encode(nbr_s, deg_s, hi_s, lo_s)
    loads[4].wait()

    def step(i, _):
        aggregate_block(i, src_s, hi_s, lo_s, tal, agg_s)
        for at, n in ((1, 0), (4, 1), (6, 2)):
            pl.when(i == at)(lambda n=n: hear(n))
        for at, turn in ((3, (0, 0, 1)), (4, (1, 0, 1)), (5, (0, 0, 0)), (6, (1, 0, 0)), (7, (0, 1, 1))):
            pl.when(i == at)(lambda turn=turn: serve(*turn))
        return 0

    lax.fori_loop(0, 8, step, 0)

    lhs[0:F] = src_s[:, 0:T]
    for j in range(8):
        at = slice(j * 256, (j + 1) * 256)
        total = agg_s[pl.ds(j, 256, stride=8), :].T
        lhs[F : 2 * F, at] = (total[0:F] / jnp.maximum(deg_s[:, at], 1).astype(jnp.float32)).astype(jnp.bfloat16)
    lhs[2 * F : 2 * F + 16] = jnp.ones((16, T), jnp.bfloat16)

    serve(1, 1, 1)
    hear(3)
    add(0, 0)
    serve(0, 1, 0)
    serve(1, 1, 0)
    add(-1, 1)
    add(1, 4)
    serve(0, 2, 1)
    serve(1, 2, 1)
    add(-2, 2)
    add(2, 5)
    serve(0, 2, 0)
    serve(1, 2, 0)
    add(-3, 3)
    add(3, 6)
    serve(0, 3, 1)
    serve(1, 3, 1)
    add(4, 7)

    bias = jnp.concatenate([acc[2 * F : 2 * F + 1, b * 128 : (b + 1) * 128] for b in range(8)], axis=0)
    for a in range(4):
        for b in range(8):
            rows = acc[a * 24 : a * 24 + 24, b * 128 : (b + 1) * 128]
            part[a * 8 + b] = jnp.concatenate([rows, bias], axis=0).astype(jnp.bfloat16)

    hear(4)

    def scatter(n):
        half = pl.ds(n * 16, 16)
        for p in PEERS:
            pltpu.make_async_remote_copy(
                src_ref=part.at[peer(*p), half], dst_ref=rs.at[n, dp], send_sem=rs_send.at[n], recv_sem=rs_recv.at[n],
                device_id=(peer(*p), col), device_id_type=MESH,
            ).start()
        rs[n, dp] = part[dp, n * 16 : n * 16 + 16]

    scale = jnp.float32(1.0) / jnp.sqrt(jnp.float32(T * NDP))
    cols = pl.ds(pl.multiple_of(dp % 8 * 128, 128), 128)

    def spread(n):
        every = rs.at[n, pl.ds(0, NP)]
        pltpu.make_async_copy(every, every, rs_recv.at[n]).wait()
        total = rs[n, 0].astype(jnp.float32)
        for d in range(1, NDP):
            total += rs[n, d].astype(jnp.float32)
        total *= scale
        size = 16 - 8 * n
        rows = pl.ds(pl.multiple_of(dp // 8 * 24 + n * 16, 8), size)
        mine[n] = total
        for p in PEERS:
            pltpu.make_async_remote_copy(
                src_ref=mine.at[n, pl.ds(0, size)], dst_ref=grad_ref.at[rows, cols], send_sem=ag_send.at[n],
                recv_sem=ag_recv.at[n], device_id=(peer(*p), col), device_id_type=MESH,
            ).start()
        own = pltpu.make_async_copy(mine.at[n, pl.ds(0, size)], grad_ref.at[rows, cols], own_sem.at[n])
        own.start()
        return own

    scatter(0)
    scatter(1)
    owns = [spread(0), spread(1)]
    bias_ref[...] = mine[1, 8:16]

    for q in range(C):
        for s in range(4):
            for far in (1, 0) if s < 3 else (1,):
                up(q, s, far, col).wait_send()
                dn(q, s, far, col).wait_send()
        for i in range(8):
            sib(q, i, col).wait_send()
    for n in range(2):
        sent, every = rs.at[n, pl.ds(0, NP)], agg_s.at[pl.ds(0, NP * (16 - 8 * n))]
        pltpu.make_async_copy(sent, sent, rs_send.at[n]).wait()
        owns[n].wait()
        pltpu.make_async_copy(every, every, ag_send.at[n]).wait()
    for n in range(2):
        every = agg_s.at[pl.ds(0, NP * (16 - 8 * n))]
        pltpu.make_async_copy(every, every, ag_recv.at[n]).wait()


def place(grad_ref, bias_ref, self_ref, neigh_ref, out_ref):
    self_ref[...] = grad_ref[0:F]
    neigh_ref[...] = grad_ref[F : 2 * F]
    out_ref[...] = bias_ref[...]


def per_device(source_feats, neighbours, degree, counts, upstream, preact):
    any_, vmem = pl.BlockSpec(memory_space=pl.ANY), pl.BlockSpec(memory_space=pltpu.VMEM)
    dma = pltpu.SemaphoreType.DMA
    f32, bf16, i32 = jnp.float32, jnp.bfloat16, jnp.int32
    grad, bias = pl.pallas_call(
        kernel,
        out_shape=(jax.ShapeDtypeStruct((2 * F, H), f32), jax.ShapeDtypeStruct((8, 128), f32)),
        in_specs=[any_, any_, any_, pl.BlockSpec(memory_space=pltpu.SMEM), any_, any_],
        out_specs=(any_, vmem),
        scratch_shapes=[
            pltpu.VMEM((F, 4096), bf16),
            pltpu.VMEM((25, T), i32),
            pltpu.VMEM((1, T), i32),
            pltpu.VMEM((ROWS, H), bf16),
            pltpu.VMEM((ROWS, H), bf16),
            pltpu.VMEM((256, 256), f32),
            pltpu.VMEM((256, 256), f32),
            pltpu.VMEM((16, 256, 256), bf16),
            pltpu.VMEM((T, 128), f32),
            pltpu.VMEM((2 * F + 16, T), bf16),
            pltpu.VMEM((C, NCOL, ROWS, W), bf16),
            pltpu.VMEM((2 * F + 16, H), f32),
            pltpu.VMEM((NDP, 32, 128), bf16),
            pltpu.VMEM((2, NDP, 16, 128), bf16),
            pltpu.VMEM((2, 16, 128), f32),
            dma((5,)),
            dma((C * 8,)), dma((C * 8,)), dma((C * 8,)), dma((C * 8,)), dma((C, 8)), dma((C, 8)),
            dma((2,)), dma((2,)), dma((2,)), dma((2,)), dma((2,)), pltpu.SemaphoreType.REGULAR((NY // 2 + 1,)),
        ],
        compiler_params=pltpu.CompilerParams(collective_id=0, has_side_effects=True, vmem_limit_bytes=60 << 20),
        name="sage_grads",
    )(source_feats, neighbours.T, degree.reshape(1, T), counts, upstream, preact)
    own, neigh, bias = pl.pallas_call(
        place,
        out_shape=(jax.ShapeDtypeStruct((F, H), f32), jax.ShapeDtypeStruct((F, H), f32), jax.ShapeDtypeStruct((8, 128), f32)),
        in_specs=[vmem, vmem],
        out_specs=(vmem, vmem, vmem),
        compiler_params=pltpu.CompilerParams(vmem_limit_bytes=60 << 20),
        name="place",
    )(grad, bias)
    return own, neigh, bias.reshape(H)


def solution(mesh):
    placed = (P("col", "dp"), P("dp", None), P("dp"), P("dp"), P(("dp", "col"), None), P(("dp", "col"), None))
    return jax.shard_map(
        per_device,
        mesh=mesh,
        in_specs=placed,
        out_specs=(P("col", None), P("col", None), P()),
        check_vma=False,
    )
```

```python
import jax
import jax.numpy as jnp
from jax import lax
from jax.experimental import pallas as pl
from jax.experimental.pallas import tpu as pltpu
from jax.sharding import PartitionSpec as P

MESH = pl.DeviceIdType.MESH
NT = (((1,), (1,)), ((), ()))
NZ, NY, NX = 8, 8, 4
NDP, NCOL = NY * NX, NZ * 2
C = 2
H = 1024
W = H // C
ROWS = 128
T = 2048
F = 48
NP = NDP - 1
ONEHOT = jnp.float8_e4m3fn
PEERS = sorted(
    ((dy, dx) for dy in range(NY) for dx in range(NX) if dy or dx),
    key=lambda p: -(min(p[0], NY - p[0]) + min(p[1], NX - p[1])),
)


def encode(nbr_ref, deg_ref, hi_s, lo_s):
    k, t = nbr_ref.shape
    nb = nbr_ref[...]
    live = lax.broadcasted_iota(jnp.int32, (k, t), 0) < deg_ref[...]
    j = lax.broadcasted_iota(jnp.int32, (k, t), 1) // 256
    hi = jnp.where(live, (nb >> 8) * 8 + j, 255).astype(jnp.float32)
    lo = (nb & 255).astype(jnp.float32)
    pad = jnp.full((32 - k, t), 255.0, jnp.float32)
    for code, out in ((hi, hi_s), (lo, lo_s)):
        code = jnp.concatenate([code, pad], axis=0)
        out[...] = jnp.concatenate([code[:, i * 256 : (i + 1) * 256] for i in range(8)], axis=0).T


def tally(hi_s, lo_s, g, rows_hi, rows_lo):
    one, zero = jnp.ones((), jnp.bfloat16), jnp.zeros((), jnp.bfloat16)
    h = jnp.broadcast_to(hi_s[pl.ds(g, 1), :], (16, 256)).astype(jnp.bfloat16)
    l = jnp.broadcast_to(lo_s[pl.ds(g, 1), :], (16, 256)).astype(jnp.bfloat16)
    left = jnp.where(rows_hi == h[None], one, zero).reshape(128, 256).astype(ONEHOT)
    right = jnp.where(rows_lo == l[None], one, zero).reshape(256, 256).astype(ONEHOT)
    return lax.dot_general(left, right, NT, preferred_element_type=jnp.float32)


def aggregate_block(b, src_s, hi_s, lo_s, tal, agg_s):
    def rows(n):
        ids = lax.broadcasted_iota(jnp.int32, (n, 256), 0).astype(jnp.float32)
        return ids.astype(jnp.bfloat16).reshape(n // 16, 16, 256)

    rows_hi, rows_lo = rows(128), rows(256)

    def pair(p, _):
        g = b * 32 + p * 2
        first = tally(hi_s, lo_s, g, rows_hi, rows_lo).reshape(16, 1, 8, 256)
        second = tally(hi_s, lo_s, g + 1, rows_hi, rows_lo).reshape(16, 1, 8, 256)
        both = jnp.concatenate([first, second], axis=1).reshape(16, 16, 256)
        tal[:, pl.ds(pl.multiple_of(p * 16, 16), 16), :] = both.astype(jnp.bfloat16)
        return 0

    lax.fori_loop(0, 16, pair, 0, unroll=16)
    total = jnp.zeros((256, F), jnp.float32)
    for h in range(16):
        total += lax.dot_general(tal[h], src_s[:, h * 256 : (h + 1) * 256], NT, preferred_element_type=jnp.float32)
    agg_s[pl.ds(pl.multiple_of(b * 256, 256), 256), 0:F] = total


def kernel(
    src_hbm, nbr_hbm, deg_hbm, counts_ref, up_hbm, pre_hbm,
    grad_ref, bias_ref,
    src_s, nbr_s, deg_s, up_s, pre_s, hi_s, lo_s, tal, agg_s, lhs, dz, acc, part, rs, mine, stage,
    load_sem, up_send, up_recv, dn_send, dn_recv, sib_send, sib_recv, rs_send, rs_recv, y_send, y_recv, x_send, x_recv, own_sem, news,
):
    dp, col = lax.axis_index("dp"), lax.axis_index("col")
    y, x, z, core = dp // NX, dp % NX, col // 2, col % 2
    above, below = (z + 1) % NZ * 2 + core, (z + NZ - 1) % NZ * 2 + core
    sibling = z * 2 + 1 - core

    def peer(dy, dx):
        return (y + dy) % NY * NX + (x + dx) % NX

    barrier = pltpu.get_barrier_semaphore()
    beside_x, beside_y = (peer(0, 1), peer(0, NX - 1)), (peer(1, 0), peer(NY - 1, 0))
    near = [(dp, above), (dp, below), (dp, sibling)] + [(p, col) for p in beside_x + beside_y]
    for to in near:
        pl.semaphore_signal(barrier, inc=1, device_id=to, device_id_type=MESH)

    loads = [
        pltpu.make_async_copy(a, b, load_sem.at[i])
        for i, (a, b) in enumerate(
            ((up_hbm, up_s), (pre_hbm, pre_s), (nbr_hbm, nbr_s), (deg_hbm, deg_s), (src_hbm, src_s))
        )
    ]
    for load in loads:
        load.start()


    loads[0].wait()
    loads[1].wait()
    limit = counts_ref[0]
    row = col * ROWS + lax.broadcasted_iota(jnp.int32, (ROWS, W), 0)
    for q in range(C):
        at = slice(q * W, (q + 1) * W)
        keep = (pre_s[:, at].astype(jnp.float32) > 0) & (row < limit)
        dz[q, col] = jnp.where(keep, up_s[:, at].astype(jnp.float32), 0.0).astype(jnp.bfloat16)

    pl.semaphore_wait(barrier, len(near))

    def tell(n):
        for to in beside_x if n == 0 else beside_y:
            pl.semaphore_signal(news.at[n], inc=1, device_id=(to, col), device_id_type=MESH)

    def hear(n):
        pl.semaphore_wait(news.at[n], 2)
        if n < NY // 2:
            tell(n + 1)

    tell(0)

    def send(ref, send_sem, recv_sem, to):
        return pltpu.make_async_remote_copy(
            src_ref=ref, dst_ref=ref, send_sem=send_sem, recv_sem=recv_sem, device_id=to, device_id_type=MESH
        )

    halves = pl.ds(0, ROWS // 2), pl.ds(ROWS // 2, ROWS // 2)

    def up(q, s, far, slot):
        n = q * 8 + s * 2 + far
        return send(dz.at[q, slot, halves[1 - far]], up_send.at[n], up_recv.at[n], (dp, above))

    def dn(q, s, far, slot):
        n = q * 8 + s * 2 + far
        return send(dz.at[q, slot, halves[far]], dn_send.at[n], dn_recv.at[n], (dp, below))

    def sib(q, i, slot):
        return send(dz.at[q, slot], sib_send.at[q, i], sib_recv.at[q, i], (dp, sibling))

    for far in (1, 0):
        for q in range(C):
            up(q, 0, far, col).start()
            dn(q, 0, far, col).start()
    for q in range(C):
        sib(q, 0, col).start()

    def serve(q, s, far):
        from_below = (z + NZ - 1 - s) % NZ * 2 + core
        from_above = (z + 1 + s) % NZ * 2 + core
        onward = s < 2 + far
        up(q, s, far, from_below).wait_recv()
        if onward:
            up(q, s + 1, far, from_below).start()
        dn(q, s, far, from_above).wait_recv()
        if onward:
            dn(q, s + 1, far, from_above).start()
        if s == 3:
            sib(q, 7, from_below).start()
        elif not far:
            sib(q, s + 1, from_below).start()
            sib(q, s + 4, from_above).start()

    def add(dz_, i):
        at = (z + NZ + dz_) % NZ
        for q in range(C):
            sib(q, i, at * 2 + 1 - core).wait_recv()
        rows = lhs[:, pl.ds(pl.multiple_of(at * 2 * ROWS, 2 * ROWS), 2 * ROWS)]
        for q in range(C):
            new = jnp.dot(rows, dz[q, pl.ds(at * 2, 2)].reshape(2 * ROWS, W), preferred_element_type=jnp.float32)
            here = slice(q * W, (q + 1) * W)
            acc[:, here] = new if dz_ == 0 else acc[:, here] + new

    loads[2].wait()
    loads[3].wait()
    encode(nbr_s, deg_s, hi_s, lo_s)
    loads[4].wait()

    def step(i, _):
        aggregate_block(i, src_s, hi_s, lo_s, tal, agg_s)
        for at, turn in ((3, (0, 0, 1)), (4, (1, 0, 1)), (5, (0, 0, 0)), (6, (1, 0, 0)), (7, (0, 1, 1))):
            pl.when(i == at)(lambda turn=turn: serve(*turn))
        for at, n in ((3, 0), (5, 1), (7, 2)):
            pl.when(i == at)(lambda n=n: hear(n))
        return 0

    lax.fori_loop(0, 8, step, 0)

    lhs[0:F] = src_s[:, 0:T]
    for j in range(8):
        at = slice(j * 256, (j + 1) * 256)
        total = agg_s[pl.ds(j, 256, stride=8), :].T
        lhs[F : 2 * F, at] = (total[0:F] / jnp.maximum(deg_s[:, at], 1).astype(jnp.float32)).astype(jnp.bfloat16)
    lhs[2 * F : 2 * F + 16] = jnp.ones((16, T), jnp.bfloat16)

    serve(1, 1, 1)
    hear(3)
    add(0, 0)
    serve(0, 1, 0)
    serve(1, 1, 0)
    add(-1, 1)
    add(1, 4)
    serve(0, 2, 1)
    serve(1, 2, 1)
    add(-2, 2)
    add(2, 5)
    serve(0, 2, 0)
    serve(1, 2, 0)
    add(-3, 3)
    add(3, 6)
    serve(0, 3, 1)
    serve(1, 3, 1)
    add(4, 7)

    bias = jnp.concatenate([acc[2 * F : 2 * F + 1, b * 128 : (b + 1) * 128] for b in range(8)], axis=0)
    for a in range(4):
        for b in range(8):
            rows = acc[a * 24 : a * 24 + 24, b * 128 : (b + 1) * 128]
            part[a * 8 + b] = jnp.concatenate([rows, bias], axis=0).astype(jnp.bfloat16)

    hear(4)

    def scatter(n):
        half = pl.ds(n * 16, 16)
        for p in PEERS:
            pltpu.make_async_remote_copy(
                src_ref=part.at[peer(*p), half], dst_ref=rs.at[n, dp], send_sem=rs_send.at[n], recv_sem=rs_recv.at[n],
                device_id=(peer(*p), col), device_id_type=MESH,
            ).start()
        rs[n, dp] = part[dp, n * 16 : n * 16 + 16]

    scale = jnp.float32(1.0) / jnp.sqrt(jnp.float32(T * NDP))

    def tile(owner, n):
        rows = pl.ds(pl.multiple_of(owner // 8 * 24 + n * 16, 8), 16 - 8 * n)
        return grad_ref.at[rows, pl.ds(pl.multiple_of(owner % 8 * 128, 128), 128)]

    def along_x(ref, owner, n):
        for dx in (2, 1, 3):
            pltpu.make_async_remote_copy(
                src_ref=ref, dst_ref=tile(owner, n), send_sem=x_send.at[n], recv_sem=x_recv.at[n],
                device_id=(peer(0, dx), col), device_id_type=MESH,
            ).start()
        pltpu.make_async_copy(ref, tile(owner, n), own_sem.at[n]).start()

    def along_y(n, dy):
        return pltpu.make_async_remote_copy(
            src_ref=mine.at[n, pl.ds(0, 16 - 8 * n)], dst_ref=stage.at[n, dy, pl.ds(0, 16 - 8 * n)],
            send_sem=y_send.at[n], recv_sem=y_recv.at[n * NY + dy], device_id=(peer(dy, 0), col), device_id_type=MESH,
        )

    def spread(n):
        every = rs.at[n, pl.ds(0, NP)]
        pltpu.make_async_copy(every, every, rs_recv.at[n]).wait()
        total = rs[n, 0].astype(jnp.float32)
        for d in range(1, NDP):
            total += rs[n, d].astype(jnp.float32)
        mine[n] = total * scale
        for dy in (4, 3, 5, 2, 6, 1, 7):
            along_y(n, dy).start()
        along_x(mine.at[n, pl.ds(0, 16 - 8 * n)], dp, n)

    def pass_on(n):
        for dy in (1, 7, 2, 6, 3, 5, 4):
            along_y(n, dy).wait_recv()
            along_x(stage.at[n, dy, pl.ds(0, 16 - 8 * n)], peer(NY - dy, 0), n)

    scatter(0)
    scatter(1)
    spread(0)
    spread(1)
    pass_on(0)
    pass_on(1)
    bias_ref[...] = mine[1, 8:16]

    for q in range(C):
        for s in range(4):
            for far in (1, 0) if s < 3 else (1,):
                up(q, s, far, col).wait_send()
                dn(q, s, far, col).wait_send()
        for i in range(8):
            sib(q, i, col).wait_send()
    def as_many(tiles, n):
        return agg_s.at[pl.ds(0, tiles * (16 - 8 * n))]

    for n in range(2):
        sent = rs.at[n, pl.ds(0, NP)]
        pltpu.make_async_copy(sent, sent, rs_send.at[n]).wait()
        for sem, tiles in ((y_send, NY - 1), (own_sem, NY), (x_send, NY * (NX - 1)), (x_recv, NY * (NX - 1))):
            pltpu.make_async_copy(as_many(tiles, n), as_many(tiles, n), sem.at[n]).wait()


def place(grad_ref, bias_ref, self_ref, neigh_ref, out_ref):
    self_ref[...] = grad_ref[0:F]
    neigh_ref[...] = grad_ref[F : 2 * F]
    out_ref[...] = bias_ref[...]


def per_device(source_feats, neighbours, degree, counts, upstream, preact):
    any_, vmem = pl.BlockSpec(memory_space=pl.ANY), pl.BlockSpec(memory_space=pltpu.VMEM)
    dma = pltpu.SemaphoreType.DMA
    f32, bf16, i32 = jnp.float32, jnp.bfloat16, jnp.int32
    grad, bias = pl.pallas_call(
        kernel,
        out_shape=(jax.ShapeDtypeStruct((2 * F, H), f32), jax.ShapeDtypeStruct((8, 128), f32)),
        in_specs=[any_, any_, any_, pl.BlockSpec(memory_space=pltpu.SMEM), any_, any_],
        out_specs=(any_, vmem),
        scratch_shapes=[
            pltpu.VMEM((F, 4096), bf16),
            pltpu.VMEM((25, T), i32),
            pltpu.VMEM((1, T), i32),
            pltpu.VMEM((ROWS, H), bf16),
            pltpu.VMEM((ROWS, H), bf16),
            pltpu.VMEM((256, 256), f32),
            pltpu.VMEM((256, 256), f32),
            pltpu.VMEM((16, 256, 256), bf16),
            pltpu.VMEM((T, 128), f32),
            pltpu.VMEM((2 * F + 16, T), bf16),
            pltpu.VMEM((C, NCOL, ROWS, W), bf16),
            pltpu.VMEM((2 * F + 16, H), f32),
            pltpu.VMEM((NDP, 32, 128), bf16),
            pltpu.VMEM((2, NDP, 16, 128), bf16),
            pltpu.VMEM((2, 16, 128), f32),
            pltpu.VMEM((2, NY, 16, 128), f32),
            dma((5,)),
            dma((C * 8,)), dma((C * 8,)), dma((C * 8,)), dma((C * 8,)), dma((C, 8)), dma((C, 8)),
            dma((2,)), dma((2,)), dma((2,)), dma((2 * NY,)), dma((2,)), dma((2,)), dma((2,)), pltpu.SemaphoreType.REGULAR((NY // 2 + 1,)),
        ],
        compiler_params=pltpu.CompilerParams(collective_id=0, has_side_effects=True, vmem_limit_bytes=60 << 20),
        name="sage_grads",
    )(source_feats, neighbours.T, degree.reshape(1, T), counts, upstream, preact)
    own, neigh, bias = pl.pallas_call(
        place,
        out_shape=(jax.ShapeDtypeStruct((F, H), f32), jax.ShapeDtypeStruct((F, H), f32), jax.ShapeDtypeStruct((8, 128), f32)),
        in_specs=[vmem, vmem],
        out_specs=(vmem, vmem, vmem),
        compiler_params=pltpu.CompilerParams(vmem_limit_bytes=60 << 20),
        name="place",
    )(grad, bias)
    return own, neigh, bias.reshape(H)


def solution(mesh):
    placed = (P("col", "dp"), P("dp", None), P("dp"), P("dp"), P(("dp", "col"), None), P(("dp", "col"), None))
    return jax.shard_map(
        per_device,
        mesh=mesh,
        in_specs=placed,
        out_specs=(P("col", None), P("col", None), P()),
        check_vma=False,
    )
```

```python
import jax
import jax.numpy as jnp
from jax import lax
from jax.experimental import pallas as pl
from jax.experimental.pallas import tpu as pltpu
from jax.sharding import PartitionSpec as P

MESH = pl.DeviceIdType.MESH
NT = (((1,), (1,)), ((), ()))
NZ, NY, NX = 8, 8, 4
NDP, NCOL = NY * NX, NZ * 2
C = 2
H = 1024
W = H // C
ROWS = 128
T = 2048
F = 48
NP = NDP - 1
ONEHOT = jnp.float8_e4m3fn
PEERS = sorted(
    ((dy, dx) for dy in range(NY) for dx in range(NX) if dy or dx),
    key=lambda p: -(min(p[0], NY - p[0]) + min(p[1], NX - p[1])),
)


def encode(nbr_ref, deg_ref, hi_s, lo_s):
    k, t = nbr_ref.shape
    nb = nbr_ref[...]
    live = lax.broadcasted_iota(jnp.int32, (k, t), 0) < deg_ref[...]
    j = lax.broadcasted_iota(jnp.int32, (k, t), 1) // 256
    hi = jnp.where(live, (nb >> 8) * 8 + j, 255).astype(jnp.float32)
    lo = (nb & 255).astype(jnp.float32)
    pad = jnp.full((32 - k, t), 255.0, jnp.float32)
    for code, out in ((hi, hi_s), (lo, lo_s)):
        code = jnp.concatenate([code, pad], axis=0)
        out[...] = jnp.concatenate([code[:, i * 256 : (i + 1) * 256] for i in range(8)], axis=0).T


def tally(hi_s, lo_s, g, rows_hi, rows_lo):
    one, zero = jnp.ones((), jnp.bfloat16), jnp.zeros((), jnp.bfloat16)
    h = jnp.broadcast_to(hi_s[pl.ds(g, 1), :], (16, 256)).astype(jnp.bfloat16)
    l = jnp.broadcast_to(lo_s[pl.ds(g, 1), :], (16, 256)).astype(jnp.bfloat16)
    left = jnp.where(rows_hi == h[None], one, zero).reshape(128, 256).astype(ONEHOT)
    right = jnp.where(rows_lo == l[None], one, zero).reshape(256, 256).astype(ONEHOT)
    return lax.dot_general(left, right, NT, preferred_element_type=jnp.float32)


def aggregate_block(b, src_s, hi_s, lo_s, tal, agg_s):
    def rows(n):
        ids = lax.broadcasted_iota(jnp.int32, (n, 256), 0).astype(jnp.float32)
        return ids.astype(jnp.bfloat16).reshape(n // 16, 16, 256)

    rows_hi, rows_lo = rows(128), rows(256)

    def pair(p, _):
        g = b * 32 + p * 2
        first = tally(hi_s, lo_s, g, rows_hi, rows_lo).reshape(16, 1, 8, 256)
        second = tally(hi_s, lo_s, g + 1, rows_hi, rows_lo).reshape(16, 1, 8, 256)
        both = jnp.concatenate([first, second], axis=1).reshape(16, 16, 256)
        tal[:, pl.ds(pl.multiple_of(p * 16, 16), 16), :] = both.astype(jnp.bfloat16)
        return 0

    lax.fori_loop(0, 16, pair, 0, unroll=16)
    total = jnp.zeros((256, F), jnp.float32)
    for h in range(16):
        total += lax.dot_general(tal[h], src_s[:, h * 256 : (h + 1) * 256], NT, preferred_element_type=jnp.float32)
    agg_s[pl.ds(pl.multiple_of(b * 256, 256), 256), 0:F] = total


def kernel(
    src_hbm, nbr_hbm, deg_hbm, counts_ref, up_hbm, pre_hbm,
    grad_ref, bias_ref,
    src_s, nbr_s, deg_s, up_s, pre_s, hi_s, lo_s, tal, agg_s, lhs, dz, acc, part, rs, mine, stage,
    load_sem, up_send, up_recv, dn_send, dn_recv, sib_send, sib_recv, rs_send, rs_recv, y_send, y_recv, x_send, x_recv, own_sem, news,
):
    dp, col = lax.axis_index("dp"), lax.axis_index("col")
    y, x, z, core = dp // NX, dp % NX, col // 2, col % 2
    above, below = (z + 1) % NZ * 2 + core, (z + NZ - 1) % NZ * 2 + core
    sibling = z * 2 + 1 - core

    def peer(dy, dx):
        return (y + dy) % NY * NX + (x + dx) % NX

    barrier = pltpu.get_barrier_semaphore()
    beside_x, beside_y = (peer(0, 1), peer(0, NX - 1)), (peer(1, 0), peer(NY - 1, 0))
    near = [(dp, above), (dp, below), (dp, sibling)] + [(p, col) for p in beside_x + beside_y]
    for to in near:
        pl.semaphore_signal(barrier, inc=1, device_id=to, device_id_type=MESH)

    loads = [
        pltpu.make_async_copy(a, b, load_sem.at[i])
        for i, (a, b) in enumerate(
            ((up_hbm, up_s), (pre_hbm, pre_s), (nbr_hbm, nbr_s), (deg_hbm, deg_s), (src_hbm, src_s))
        )
    ]
    for load in loads:
        load.start()


    loads[0].wait()
    loads[1].wait()
    limit = counts_ref[0]
    row = col * ROWS + lax.broadcasted_iota(jnp.int32, (ROWS, W), 0)
    for q in range(C):
        at = slice(q * W, (q + 1) * W)
        keep = (pre_s[:, at].astype(jnp.float32) > 0) & (row < limit)
        dz[q, col] = jnp.where(keep, up_s[:, at].astype(jnp.float32), 0.0).astype(jnp.bfloat16)

    pl.semaphore_wait(barrier, len(near))

    def tell(n):
        for to in beside_x if n == 0 else beside_y:
            pl.semaphore_signal(news.at[n], inc=1, device_id=(to, col), device_id_type=MESH)

    def hear(n):
        pl.semaphore_wait(news.at[n], 2)
        if n < NY // 2:
            tell(n + 1)

    tell(0)

    def send(ref, send_sem, recv_sem, to):
        return pltpu.make_async_remote_copy(
            src_ref=ref, dst_ref=ref, send_sem=send_sem, recv_sem=recv_sem, device_id=to, device_id_type=MESH
        )

    halves = pl.ds(0, ROWS // 2), pl.ds(ROWS // 2, ROWS // 2)

    def up(q, s, far, slot):
        n = q * 8 + s * 2 + far
        return send(dz.at[q, slot, halves[1 - far]], up_send.at[n], up_recv.at[n], (dp, above))

    def dn(q, s, far, slot):
        n = q * 8 + s * 2 + far
        return send(dz.at[q, slot, halves[far]], dn_send.at[n], dn_recv.at[n], (dp, below))

    def sib(q, i, slot):
        return send(dz.at[q, slot], sib_send.at[q, i], sib_recv.at[q, i], (dp, sibling))

    for far in (1, 0):
        for q in range(C):
            up(q, 0, far, col).start()
            dn(q, 0, far, col).start()
    for q in range(C):
        sib(q, 0, col).start()

    def serve(q, s, far):
        from_below = (z + NZ - 1 - s) % NZ * 2 + core
        from_above = (z + 1 + s) % NZ * 2 + core
        onward = s < 2 + far
        up(q, s, far, from_below).wait_recv()
        if onward:
            up(q, s + 1, far, from_below).start()
        dn(q, s, far, from_above).wait_recv()
        if onward:
            dn(q, s + 1, far, from_above).start()
        if s == 3:
            sib(q, 7, from_below).start()
        elif not far:
            sib(q, s + 1, from_below).start()
            sib(q, s + 4, from_above).start()

    def add(dz_, i, chunks=range(C)):
        at = (z + NZ + dz_) % NZ
        rows = lhs[:, pl.ds(pl.multiple_of(at * 2 * ROWS, 2 * ROWS), 2 * ROWS)]
        for q in chunks:
            sib(q, i, at * 2 + 1 - core).wait_recv()
            new = jnp.dot(rows, dz[q, pl.ds(at * 2, 2)].reshape(2 * ROWS, W), preferred_element_type=jnp.float32)
            here = slice(q * W, (q + 1) * W)
            acc[:, here] = new if dz_ == 0 else acc[:, here] + new

    loads[2].wait()
    loads[3].wait()
    encode(nbr_s, deg_s, hi_s, lo_s)
    loads[4].wait()

    def step(i, _):
        aggregate_block(i, src_s, hi_s, lo_s, tal, agg_s)
        for at, turn in ((2, (0, 0, 1)), (3, (1, 0, 1)), (4, (0, 0, 0)), (5, (1, 0, 0)), (6, (0, 1, 1)), (7, (1, 1, 1))):
            pl.when(i == at)(lambda turn=turn: serve(*turn))
        for at, n in ((3, 0), (5, 1), (7, 2)):
            pl.when(i == at)(lambda n=n: hear(n))
        return 0

    lax.fori_loop(0, 8, step, 0)

    lhs[0:F] = src_s[:, 0:T]
    for j in range(8):
        at = slice(j * 256, (j + 1) * 256)
        total = agg_s[pl.ds(j, 256, stride=8), :].T
        lhs[F : 2 * F, at] = (total[0:F] / jnp.maximum(deg_s[:, at], 1).astype(jnp.float32)).astype(jnp.bfloat16)
    lhs[2 * F : 2 * F + 16] = jnp.ones((16, T), jnp.bfloat16)

    hear(3)
    add(0, 0)
    serve(0, 1, 0)
    serve(1, 1, 0)
    add(-1, 1)
    add(1, 4)
    serve(0, 2, 1)
    serve(1, 2, 1)
    add(-2, 2)
    add(2, 5)
    serve(0, 2, 0)
    serve(1, 2, 0)
    add(-3, 3)
    add(3, 6)

    for q in range(C):
        serve(q, 3, 1)
        add(4, 7, (q,))
        for b in range(q * 8 // C, (q + 1) * 8 // C):
            at = slice(b * 128, (b + 1) * 128)
            for a in range(4):
                part[a * 8 + b, 0:16] = acc[a * 24 : a * 24 + 16, at].astype(jnp.bfloat16)
    bias = jnp.concatenate([acc[2 * F : 2 * F + 1, b * 128 : (b + 1) * 128] for b in range(8)], axis=0)

    def finish_part():
        for b in range(8):
            at = slice(b * 128, (b + 1) * 128)
            for a in range(4):
                rows = acc[a * 24 + 16 : a * 24 + 24, at]
                part[a * 8 + b, 16:32] = jnp.concatenate([rows, bias], axis=0).astype(jnp.bfloat16)

    hear(4)

    def scatter(n):
        half = pl.ds(n * 16, 16)
        for p in PEERS:
            pltpu.make_async_remote_copy(
                src_ref=part.at[peer(*p), half], dst_ref=rs.at[n, dp], send_sem=rs_send.at[n], recv_sem=rs_recv.at[n],
                device_id=(peer(*p), col), device_id_type=MESH,
            ).start()
        rs[n, dp] = part[dp, n * 16 : n * 16 + 16]

    scale = jnp.float32(1.0) / jnp.sqrt(jnp.float32(T * NDP))

    def tile(owner, n):
        rows = pl.ds(pl.multiple_of(owner // 8 * 24 + n * 16, 8), 16 - 8 * n)
        return grad_ref.at[rows, pl.ds(pl.multiple_of(owner % 8 * 128, 128), 128)]

    def along_x(ref, owner, n):
        for dx in (2, 1, 3):
            pltpu.make_async_remote_copy(
                src_ref=ref, dst_ref=tile(owner, n), send_sem=x_send.at[n], recv_sem=x_recv.at[n],
                device_id=(peer(0, dx), col), device_id_type=MESH,
            ).start()
        pltpu.make_async_copy(ref, tile(owner, n), own_sem.at[n]).start()

    def along_y(n, dy):
        return pltpu.make_async_remote_copy(
            src_ref=mine.at[n, pl.ds(0, 16 - 8 * n)], dst_ref=stage.at[n, dy, pl.ds(0, 16 - 8 * n)],
            send_sem=y_send.at[n], recv_sem=y_recv.at[n * NY + dy], device_id=(peer(dy, 0), col), device_id_type=MESH,
        )

    def spread(n):
        every = rs.at[n, pl.ds(0, NP)]
        pltpu.make_async_copy(every, every, rs_recv.at[n]).wait()
        total = rs[n, 0].astype(jnp.float32)
        for d in range(1, NDP):
            total += rs[n, d].astype(jnp.float32)
        mine[n] = total * scale
        if n == 1:
            for p in PEERS:
                pltpu.make_async_remote_copy(
                    src_ref=mine.at[n, pl.ds(0, 8)], dst_ref=tile(dp, n), send_sem=x_send.at[n], recv_sem=x_recv.at[n],
                    device_id=(peer(*p), col), device_id_type=MESH,
                ).start()
            pltpu.make_async_copy(mine.at[n, pl.ds(0, 8)], tile(dp, n), own_sem.at[n]).start()
            return
        for dy in (4, 3, 5, 2, 6, 1, 7):
            along_y(n, dy).start()
        along_x(mine.at[n, pl.ds(0, 16)], dp, n)

    def pass_on(n):
        for dy in (1, 7, 2, 6, 3, 5, 4):
            along_y(n, dy).wait_recv()
            along_x(stage.at[n, dy, pl.ds(0, 16 - 8 * n)], peer(NY - dy, 0), n)

    scatter(0)
    finish_part()
    scatter(1)
    spread(0)
    spread(1)
    pass_on(0)
    bias_ref[...] = mine[1, 8:16]

    for q in range(C):
        for s in range(4):
            for far in (1, 0) if s < 3 else (1,):
                up(q, s, far, col).wait_send()
                dn(q, s, far, col).wait_send()
        for i in range(8):
            sib(q, i, col).wait_send()
    def as_many(tiles, n):
        return agg_s.at[pl.ds(0, tiles * (16 - 8 * n))]

    for n in range(2):
        sent = rs.at[n, pl.ds(0, NP)]
        pltpu.make_async_copy(sent, sent, rs_send.at[n]).wait()
        relayed = ((y_send, NY - 1), (own_sem, NY), (x_send, NY * (NX - 1)), (x_recv, NY * (NX - 1)))
        direct = ((own_sem, 1), (x_send, NP), (x_recv, NP))
        for sem, tiles in direct if n else relayed:
            pltpu.make_async_copy(as_many(tiles, n), as_many(tiles, n), sem.at[n]).wait()


def place(grad_ref, bias_ref, self_ref, neigh_ref, out_ref):
    self_ref[...] = grad_ref[0:F]
    neigh_ref[...] = grad_ref[F : 2 * F]
    out_ref[...] = bias_ref[...]


def per_device(source_feats, neighbours, degree, counts, upstream, preact):
    any_, vmem = pl.BlockSpec(memory_space=pl.ANY), pl.BlockSpec(memory_space=pltpu.VMEM)
    dma = pltpu.SemaphoreType.DMA
    f32, bf16, i32 = jnp.float32, jnp.bfloat16, jnp.int32
    grad, bias = pl.pallas_call(
        kernel,
        out_shape=(jax.ShapeDtypeStruct((2 * F, H), f32), jax.ShapeDtypeStruct((8, 128), f32)),
        in_specs=[any_, any_, any_, pl.BlockSpec(memory_space=pltpu.SMEM), any_, any_],
        out_specs=(any_, vmem),
        scratch_shapes=[
            pltpu.VMEM((F, 4096), bf16),
            pltpu.VMEM((25, T), i32),
            pltpu.VMEM((1, T), i32),
            pltpu.VMEM((ROWS, H), bf16),
            pltpu.VMEM((ROWS, H), bf16),
            pltpu.VMEM((256, 256), f32),
            pltpu.VMEM((256, 256), f32),
            pltpu.VMEM((16, 256, 256), bf16),
            pltpu.VMEM((T, 128), f32),
            pltpu.VMEM((2 * F + 16, T), bf16),
            pltpu.VMEM((C, NCOL, ROWS, W), bf16),
            pltpu.VMEM((2 * F + 16, H), f32),
            pltpu.VMEM((NDP, 32, 128), bf16),
            pltpu.VMEM((2, NDP, 16, 128), bf16),
            pltpu.VMEM((2, 16, 128), f32),
            pltpu.VMEM((2, NY, 16, 128), f32),
            dma((5,)),
            dma((C * 8,)), dma((C * 8,)), dma((C * 8,)), dma((C * 8,)), dma((C, 8)), dma((C, 8)),
            dma((2,)), dma((2,)), dma((2,)), dma((2 * NY,)), dma((2,)), dma((2,)), dma((2,)), pltpu.SemaphoreType.REGULAR((NY // 2 + 1,)),
        ],
        compiler_params=pltpu.CompilerParams(collective_id=0, has_side_effects=True, vmem_limit_bytes=60 << 20),
        name="sage_grads",
    )(source_feats, neighbours.T, degree.reshape(1, T), counts, upstream, preact)
    own, neigh, bias = pl.pallas_call(
        place,
        out_shape=(jax.ShapeDtypeStruct((F, H), f32), jax.ShapeDtypeStruct((F, H), f32), jax.ShapeDtypeStruct((8, 128), f32)),
        in_specs=[vmem, vmem],
        out_specs=(vmem, vmem, vmem),
        compiler_params=pltpu.CompilerParams(vmem_limit_bytes=60 << 20),
        name="place",
    )(grad, bias)
    return own, neigh, bias.reshape(H)


def solution(mesh):
    placed = (P("col", "dp"), P("dp", None), P("dp"), P("dp"), P(("dp", "col"), None), P(("dp", "col"), None))
    return jax.shard_map(
        per_device,
        mesh=mesh,
        in_specs=placed,
        out_specs=(P("col", None), P("col", None), P()),
        check_vma=False,
    )
```

```python
import jax
import jax.numpy as jnp
from jax import lax
from jax.experimental import pallas as pl
from jax.experimental.pallas import tpu as pltpu
from jax.sharding import PartitionSpec as P

MESH = pl.DeviceIdType.MESH
NT = (((1,), (1,)), ((), ()))
NZ, NY, NX = 8, 8, 4
NDP, NCOL = NY * NX, NZ * 2
C = 2
H = 1024
W = H // C
ROWS = 128
T = 2048
F = 48
NP = NDP - 1
ONEHOT = jnp.float8_e4m3fn
PEERS = sorted(
    ((dy, dx) for dy in range(NY) for dx in range(NX) if dy or dx),
    key=lambda p: -(min(p[0], NY - p[0]) + min(p[1], NX - p[1])),
)


def encode(nbr_ref, deg_ref, hi_s, lo_s):
    k, t = nbr_ref.shape
    nb = nbr_ref[...]
    live = lax.broadcasted_iota(jnp.int32, (k, t), 0) < deg_ref[...]
    j = lax.broadcasted_iota(jnp.int32, (k, t), 1) // 256
    hi = jnp.where(live, (nb >> 8) * 8 + j, 255).astype(jnp.float32)
    lo = (nb & 255).astype(jnp.float32)
    pad = jnp.full((32 - k, t), 255.0, jnp.float32)
    for code, out in ((hi, hi_s), (lo, lo_s)):
        code = jnp.concatenate([code, pad], axis=0)
        out[...] = jnp.concatenate([code[:, i * 256 : (i + 1) * 256] for i in range(8)], axis=0).T


def tally(hi_s, lo_s, g, rows_hi, rows_lo):
    one, zero = jnp.ones((), jnp.bfloat16), jnp.zeros((), jnp.bfloat16)
    h = jnp.broadcast_to(hi_s[pl.ds(g, 1), :], (16, 256)).astype(jnp.bfloat16)
    l = jnp.broadcast_to(lo_s[pl.ds(g, 1), :], (16, 256)).astype(jnp.bfloat16)
    left = jnp.where(rows_hi == h[None], one, zero).reshape(128, 256).astype(ONEHOT)
    right = jnp.where(rows_lo == l[None], one, zero).reshape(256, 256).astype(ONEHOT)
    return lax.dot_general(left, right, NT, preferred_element_type=jnp.float32)


def aggregate_block(b, src_s, hi_s, lo_s, tal, agg_s):
    def rows(n):
        ids = lax.broadcasted_iota(jnp.int32, (n, 256), 0).astype(jnp.float32)
        return ids.astype(jnp.bfloat16).reshape(n // 16, 16, 256)

    rows_hi, rows_lo = rows(128), rows(256)

    def pair(p, _):
        g = b * 32 + p * 2
        first = tally(hi_s, lo_s, g, rows_hi, rows_lo).reshape(16, 1, 8, 256)
        second = tally(hi_s, lo_s, g + 1, rows_hi, rows_lo).reshape(16, 1, 8, 256)
        both = jnp.concatenate([first, second], axis=1).reshape(16, 16, 256)
        tal[:, pl.ds(pl.multiple_of(p * 16, 16), 16), :] = both.astype(jnp.bfloat16)
        return 0

    lax.fori_loop(0, 16, pair, 0, unroll=16)
    total = jnp.zeros((256, F), jnp.float32)
    for h in range(16):
        total += lax.dot_general(tal[h], src_s[:, h * 256 : (h + 1) * 256], NT, preferred_element_type=jnp.float32)
    agg_s[pl.ds(pl.multiple_of(b * 256, 256), 256), 0:F] = total


def kernel(
    src_hbm, nbr_hbm, deg_hbm, counts_ref, up_hbm, pre_hbm,
    grad_ref, bias_ref,
    src_s, nbr_s, deg_s, up_s, pre_s, hi_s, lo_s, tal, agg_s, lhs, dz, acc, part, rs, mine, stage,
    load_sem, up_send, up_recv, dn_send, dn_recv, sib_send, sib_recv, rs_send, rs_recv, y_send, y_recv, x_send, x_recv, own_sem, bias_sem, news,
):
    dp, col = lax.axis_index("dp"), lax.axis_index("col")
    y, x, z, core = dp // NX, dp % NX, col // 2, col % 2
    above, below = (z + 1) % NZ * 2 + core, (z + NZ - 1) % NZ * 2 + core
    sibling = z * 2 + 1 - core

    def peer(dy, dx):
        return (y + dy) % NY * NX + (x + dx) % NX

    barrier = pltpu.get_barrier_semaphore()
    beside_x, beside_y = (peer(0, 1), peer(0, NX - 1)), (peer(1, 0), peer(NY - 1, 0))
    near = [(dp, above), (dp, below), (dp, sibling)] + [(p, col) for p in beside_x + beside_y]
    for to in near:
        pl.semaphore_signal(barrier, inc=1, device_id=to, device_id_type=MESH)

    loads = [
        pltpu.make_async_copy(a, b, load_sem.at[i])
        for i, (a, b) in enumerate(
            ((up_hbm, up_s), (pre_hbm, pre_s), (nbr_hbm, nbr_s), (deg_hbm, deg_s), (src_hbm, src_s))
        )
    ]
    for load in loads:
        load.start()


    loads[0].wait()
    loads[1].wait()
    limit = counts_ref[0]
    row = col * ROWS + lax.broadcasted_iota(jnp.int32, (ROWS, W), 0)
    for q in range(C):
        at = slice(q * W, (q + 1) * W)
        keep = (pre_s[:, at].astype(jnp.float32) > 0) & (row < limit)
        dz[q, col] = jnp.where(keep, up_s[:, at].astype(jnp.float32), 0.0).astype(jnp.bfloat16)

    pl.semaphore_wait(barrier, len(near))

    def tell(n):
        for to in beside_x if n == 0 else beside_y:
            pl.semaphore_signal(news.at[n], inc=1, device_id=(to, col), device_id_type=MESH)

    def hear(n):
        pl.semaphore_wait(news.at[n], 2)
        if n < NY // 2:
            tell(n + 1)

    tell(0)

    def send(ref, send_sem, recv_sem, to):
        return pltpu.make_async_remote_copy(
            src_ref=ref, dst_ref=ref, send_sem=send_sem, recv_sem=recv_sem, device_id=to, device_id_type=MESH
        )

    halves = pl.ds(0, ROWS // 2), pl.ds(ROWS // 2, ROWS // 2)

    def up(q, s, far, slot):
        n = q * 8 + s * 2 + far
        return send(dz.at[q, slot, halves[1 - far]], up_send.at[n], up_recv.at[n], (dp, above))

    def dn(q, s, far, slot):
        n = q * 8 + s * 2 + far
        return send(dz.at[q, slot, halves[far]], dn_send.at[n], dn_recv.at[n], (dp, below))

    def sib(q, i, slot):
        return send(dz.at[q, slot], sib_send.at[q, i], sib_recv.at[q, i], (dp, sibling))

    for far in (1, 0):
        for q in range(C):
            up(q, 0, far, col).start()
            dn(q, 0, far, col).start()
    for q in range(C):
        sib(q, 0, col).start()

    def serve(q, s, far):
        from_below = (z + NZ - 1 - s) % NZ * 2 + core
        from_above = (z + 1 + s) % NZ * 2 + core
        onward = s < 2 + far
        up(q, s, far, from_below).wait_recv()
        if onward:
            up(q, s + 1, far, from_below).start()
        dn(q, s, far, from_above).wait_recv()
        if onward:
            dn(q, s + 1, far, from_above).start()
        if s == 3:
            sib(q, 7, from_below).start()
        elif not far:
            sib(q, s + 1, from_below).start()
            sib(q, s + 4, from_above).start()

    def add(dz_, i, chunks=range(C)):
        at = (z + NZ + dz_) % NZ
        rows = lhs[:, pl.ds(pl.multiple_of(at * 2 * ROWS, 2 * ROWS), 2 * ROWS)]
        for q in chunks:
            sib(q, i, at * 2 + 1 - core).wait_recv()
            new = jnp.dot(rows, dz[q, pl.ds(at * 2, 2)].reshape(2 * ROWS, W), preferred_element_type=jnp.float32)
            here = slice(q * W, (q + 1) * W)
            acc[:, here] = new if dz_ == 0 else acc[:, here] + new

    loads[2].wait()
    loads[3].wait()
    encode(nbr_s, deg_s, hi_s, lo_s)
    loads[4].wait()

    def step(i, _):
        aggregate_block(i, src_s, hi_s, lo_s, tal, agg_s)
        for at, turn in ((2, (0, 0, 1)), (3, (1, 0, 1)), (4, (0, 0, 0)), (5, (1, 0, 0)), (6, (0, 1, 1)), (7, (1, 1, 1))):
            pl.when(i == at)(lambda turn=turn: serve(*turn))
        for at, n in ((3, 0), (5, 1), (7, 2)):
            pl.when(i == at)(lambda n=n: hear(n))
        return 0

    lax.fori_loop(0, 8, step, 0)

    lhs[0:F] = src_s[:, 0:T]
    for j in range(8):
        at = slice(j * 256, (j + 1) * 256)
        total = agg_s[pl.ds(j, 256, stride=8), :].T
        lhs[F : 2 * F, at] = (total[0:F] / jnp.maximum(deg_s[:, at], 1).astype(jnp.float32)).astype(jnp.bfloat16)
    lhs[2 * F : 2 * F + 16] = jnp.ones((16, T), jnp.bfloat16)

    hear(3)
    add(0, 0)
    serve(0, 1, 0)
    serve(1, 1, 0)
    add(-1, 1)
    add(1, 4)
    serve(0, 2, 1)
    serve(1, 2, 1)
    add(-2, 2)
    add(2, 5)
    serve(0, 2, 0)
    serve(1, 2, 0)
    add(-3, 3)
    add(3, 6)

    for q in range(C):
        serve(q, 3, 1)
        add(4, 7, (q,))
        for b in range(q * 8 // C, (q + 1) * 8 // C):
            at = slice(b * 128, (b + 1) * 128)
            for a in range(4):
                part[a * 8 + b, 0:16] = acc[a * 24 : a * 24 + 16, at].astype(jnp.bfloat16)
    bias = jnp.concatenate([acc[2 * F : 2 * F + 1, b * 128 : (b + 1) * 128] for b in range(8)], axis=0)

    def finish_part():
        for b in range(8):
            at = slice(b * 128, (b + 1) * 128)
            for a in range(4):
                rows = acc[a * 24 + 16 : a * 24 + 24, at]
                part[a * 8 + b, 16:32] = jnp.concatenate([rows, bias], axis=0).astype(jnp.bfloat16)

    hear(4)

    def scatter(n):
        half = pl.ds(n * 16, 16)
        for p in PEERS:
            pltpu.make_async_remote_copy(
                src_ref=part.at[peer(*p), half], dst_ref=rs.at[n, dp], send_sem=rs_send.at[n], recv_sem=rs_recv.at[n],
                device_id=(peer(*p), col), device_id_type=MESH,
            ).start()
        rs[n, dp] = part[dp, n * 16 : n * 16 + 16]

    scale = jnp.float32(1.0) / jnp.sqrt(jnp.float32(T * NDP))

    def tile(owner, n):
        rows = pl.ds(pl.multiple_of(owner // 8 * 24 + n * 16, 8), 16 - 8 * n)
        return grad_ref.at[rows, pl.ds(pl.multiple_of(owner % 8 * 128, 128), 128)]

    def along_x(ref, owner, n):
        for dx in (2, 1, 3):
            pltpu.make_async_remote_copy(
                src_ref=ref, dst_ref=tile(owner, n), send_sem=x_send.at[n], recv_sem=x_recv.at[n],
                device_id=(peer(0, dx), col), device_id_type=MESH,
            ).start()
        pltpu.make_async_copy(ref, tile(owner, n), own_sem.at[n]).start()

    def along_y(n, dy):
        return pltpu.make_async_remote_copy(
            src_ref=mine.at[n, pl.ds(0, 16 - 8 * n)], dst_ref=stage.at[n, dy, pl.ds(0, 16 - 8 * n)],
            send_sem=y_send.at[n], recv_sem=y_recv.at[n * NY + dy], device_id=(peer(dy, 0), col), device_id_type=MESH,
        )

    def spread(n):
        every = rs.at[n, pl.ds(0, NP)]
        pltpu.make_async_copy(every, every, rs_recv.at[n]).wait()
        total = rs[n, 0].astype(jnp.float32)
        for d in range(1, NDP):
            total += rs[n, d].astype(jnp.float32)
        mine[n] = total * scale
        if n == 1:
            for p in PEERS:
                pltpu.make_async_remote_copy(
                    src_ref=mine.at[n, pl.ds(0, 8)], dst_ref=tile(dp, n), send_sem=x_send.at[n], recv_sem=x_recv.at[n],
                    device_id=(peer(*p), col), device_id_type=MESH,
                ).start()
            pltpu.make_async_copy(mine.at[n, pl.ds(0, 8)], tile(dp, n), own_sem.at[n]).start()
            pltpu.make_async_copy(mine.at[n, pl.ds(8, 8)], bias_ref, bias_sem).start()
            return
        for dy in (4, 3, 5, 2, 6, 1, 7):
            along_y(n, dy).start()
        along_x(mine.at[n, pl.ds(0, 16)], dp, n)

    def pass_on(n):
        for dy in (1, 7, 2, 6, 3, 5, 4):
            along_y(n, dy).wait_recv()
            along_x(stage.at[n, dy, pl.ds(0, 16 - 8 * n)], peer(NY - dy, 0), n)

    scatter(0)
    finish_part()
    scatter(1)
    spread(0)
    spread(1)
    pass_on(0)

    for q in range(C):
        for s in range(4):
            for far in (1, 0) if s < 3 else (1,):
                up(q, s, far, col).wait_send()
                dn(q, s, far, col).wait_send()
        for i in range(8):
            sib(q, i, col).wait_send()
    def as_many(tiles, n):
        return agg_s.at[pl.ds(0, tiles * (16 - 8 * n))]

    pltpu.make_async_copy(mine.at[1, pl.ds(8, 8)], bias_ref, bias_sem).wait()
    for n in range(2):
        sent = rs.at[n, pl.ds(0, NP)]
        pltpu.make_async_copy(sent, sent, rs_send.at[n]).wait()
        relayed = ((y_send, NY - 1), (own_sem, NY), (x_send, NY * (NX - 1)), (x_recv, NY * (NX - 1)))
        direct = ((own_sem, 1), (x_send, NP), (x_recv, NP))
        for sem, tiles in direct if n else relayed:
            pltpu.make_async_copy(as_many(tiles, n), as_many(tiles, n), sem.at[n]).wait()


def place(grad_ref, bias_ref, self_ref, neigh_ref, out_ref):
    self_ref[...] = grad_ref[0:F]
    neigh_ref[...] = grad_ref[F : 2 * F]
    out_ref[...] = bias_ref[...]


def per_device(source_feats, neighbours, degree, counts, upstream, preact):
    any_, vmem = pl.BlockSpec(memory_space=pl.ANY), pl.BlockSpec(memory_space=pltpu.VMEM)
    dma = pltpu.SemaphoreType.DMA
    f32, bf16, i32 = jnp.float32, jnp.bfloat16, jnp.int32
    grad, bias = pl.pallas_call(
        kernel,
        out_shape=(jax.ShapeDtypeStruct((2 * F, H), f32), jax.ShapeDtypeStruct((8, 128), f32)),
        in_specs=[any_, any_, any_, pl.BlockSpec(memory_space=pltpu.SMEM), any_, any_],
        out_specs=(any_, any_),
        scratch_shapes=[
            pltpu.VMEM((F, 4096), bf16),
            pltpu.VMEM((25, T), i32),
            pltpu.VMEM((1, T), i32),
            pltpu.VMEM((ROWS, H), bf16),
            pltpu.VMEM((ROWS, H), bf16),
            pltpu.VMEM((256, 256), f32),
            pltpu.VMEM((256, 256), f32),
            pltpu.VMEM((16, 256, 256), bf16),
            pltpu.VMEM((T, 128), f32),
            pltpu.VMEM((2 * F + 16, T), bf16),
            pltpu.VMEM((C, NCOL, ROWS, W), bf16),
            pltpu.VMEM((2 * F + 16, H), f32),
            pltpu.VMEM((NDP, 32, 128), bf16),
            pltpu.VMEM((2, NDP, 16, 128), bf16),
            pltpu.VMEM((2, 16, 128), f32),
            pltpu.VMEM((2, NY, 16, 128), f32),
            dma((5,)),
            dma((C * 8,)), dma((C * 8,)), dma((C * 8,)), dma((C * 8,)), dma((C, 8)), dma((C, 8)),
            dma((2,)), dma((2,)), dma((2,)), dma((2 * NY,)), dma((2,)), dma((2,)), dma((2,)), dma(()), pltpu.SemaphoreType.REGULAR((NY // 2 + 1,)),
        ],
        compiler_params=pltpu.CompilerParams(collective_id=0, has_side_effects=True, vmem_limit_bytes=60 << 20),
        name="sage_grads",
    )(source_feats, neighbours.T, degree.reshape(1, T), counts, upstream, preact)
    own, neigh, bias = pl.pallas_call(
        place,
        out_shape=(jax.ShapeDtypeStruct((F, H), f32), jax.ShapeDtypeStruct((F, H), f32), jax.ShapeDtypeStruct((8, 128), f32)),
        in_specs=[vmem, vmem],
        out_specs=(vmem, vmem, vmem),
        compiler_params=pltpu.CompilerParams(vmem_limit_bytes=60 << 20),
        name="place",
    )(grad, bias)
    return own, neigh, bias.reshape(H)


def solution(mesh):
    placed = (P("col", "dp"), P("dp", None), P("dp"), P("dp"), P(("dp", "col"), None), P(("dp", "col"), None))
    return jax.shard_map(
        per_device,
        mesh=mesh,
        in_specs=placed,
        out_specs=(P("col", None), P("col", None), P()),
        check_vma=False,
    )
```

```python
import jax
import jax.numpy as jnp
from jax import lax
from jax.experimental import pallas as pl
from jax.experimental.pallas import tpu as pltpu
from jax.sharding import PartitionSpec as P

MESH = pl.DeviceIdType.MESH
NT = (((1,), (1,)), ((), ()))
NZ, NY, NX = 8, 8, 4
NDP, NCOL = NY * NX, NZ * 2
C = 2
H = 1024
W = H // C
ROWS = 128
T = 2048
F = 48
NP = NDP - 1
ONEHOT = jnp.float8_e4m3fn
PEERS = sorted(
    ((dy, dx) for dy in range(NY) for dx in range(NX) if dy or dx),
    key=lambda p: -(min(p[0], NY - p[0]) + min(p[1], NX - p[1])),
)


def encode(nbr_ref, deg_ref, hi_s, lo_s):
    k, t = nbr_ref.shape
    nb = nbr_ref[...]
    live = lax.broadcasted_iota(jnp.int32, (k, t), 0) < deg_ref[...]
    j = lax.broadcasted_iota(jnp.int32, (k, t), 1) // 256
    hi = jnp.where(live, (nb >> 8) * 8 + j, 255).astype(jnp.float32)
    lo = (nb & 255).astype(jnp.float32)
    pad = jnp.full((32 - k, t), 255.0, jnp.float32)
    for code, out in ((hi, hi_s), (lo, lo_s)):
        code = jnp.concatenate([code, pad], axis=0)
        out[...] = jnp.concatenate([code[:, i * 256 : (i + 1) * 256] for i in range(8)], axis=0).T


def tally(hi_s, lo_s, g, rows_hi, rows_lo):
    one, zero = jnp.ones((), jnp.bfloat16), jnp.zeros((), jnp.bfloat16)
    h = jnp.broadcast_to(hi_s[pl.ds(g, 1), :], (16, 256)).astype(jnp.bfloat16)
    l = jnp.broadcast_to(lo_s[pl.ds(g, 1), :], (16, 256)).astype(jnp.bfloat16)
    left = jnp.where(rows_hi == h[None], one, zero).reshape(128, 256).astype(ONEHOT)
    right = jnp.where(rows_lo == l[None], one, zero).reshape(256, 256).astype(ONEHOT)
    return lax.dot_general(left, right, NT, preferred_element_type=jnp.float32)


def aggregate_block(b, src_s, hi_s, lo_s, tal, agg_s):
    def rows(n):
        ids = lax.broadcasted_iota(jnp.int32, (n, 256), 0).astype(jnp.float32)
        return ids.astype(jnp.bfloat16).reshape(n // 16, 16, 256)

    rows_hi, rows_lo = rows(128), rows(256)

    def pair(p, _):
        g = b * 32 + p * 2
        first = tally(hi_s, lo_s, g, rows_hi, rows_lo).reshape(16, 1, 8, 256)
        second = tally(hi_s, lo_s, g + 1, rows_hi, rows_lo).reshape(16, 1, 8, 256)
        both = jnp.concatenate([first, second], axis=1).reshape(16, 16, 256)
        tal[:, pl.ds(pl.multiple_of(p * 16, 16), 16), :] = both.astype(jnp.bfloat16)
        return 0

    lax.fori_loop(0, 16, pair, 0, unroll=16)
    total = jnp.zeros((256, F), jnp.float32)
    for h in range(16):
        total += lax.dot_general(tal[h], src_s[:, h * 256 : (h + 1) * 256], NT, preferred_element_type=jnp.float32)
    agg_s[pl.ds(pl.multiple_of(b * 256, 256), 256), 0:F] = total


def kernel(
    src_hbm, nbr_hbm, deg_hbm, counts_ref, up_hbm, pre_hbm,
    grad_ref, bias_ref,
    src_s, nbr_s, deg_s, up_s, pre_s, hi_s, lo_s, tal, agg_s, lhs, dz, acc, part, rs, mine, stage,
    load_sem, up_send, up_recv, dn_send, dn_recv, sib_send, sib_recv, rs_send, rs_recv, y_send, y_recv, x_send, x_recv, own_sem, bias_sem, news,
):
    dp, col = lax.axis_index("dp"), lax.axis_index("col")
    y, x, z, core = dp // NX, dp % NX, col // 2, col % 2
    above, below = (z + 1) % NZ * 2 + core, (z + NZ - 1) % NZ * 2 + core
    sibling = z * 2 + 1 - core

    def peer(dy, dx):
        return (y + dy) % NY * NX + (x + dx) % NX

    barrier = pltpu.get_barrier_semaphore()
    beside_x, beside_y = (peer(0, 1), peer(0, NX - 1)), (peer(1, 0), peer(NY - 1, 0))
    near = [(dp, above), (dp, below), (dp, sibling)] + [(p, col) for p in beside_x + beside_y]
    for to in near:
        pl.semaphore_signal(barrier, inc=1, device_id=to, device_id_type=MESH)

    loads = [
        pltpu.make_async_copy(a, b, load_sem.at[i])
        for i, (a, b) in enumerate(
            ((up_hbm, up_s), (pre_hbm, pre_s), (nbr_hbm, nbr_s), (deg_hbm, deg_s), (src_hbm, src_s))
        )
    ]
    for load in loads:
        load.start()


    loads[0].wait()
    loads[1].wait()
    limit = counts_ref[0]
    row = col * ROWS + lax.broadcasted_iota(jnp.int32, (ROWS, W), 0)
    for q in range(C):
        at = slice(q * W, (q + 1) * W)
        keep = (pre_s[:, at].astype(jnp.float32) > 0) & (row < limit)
        dz[q, col] = jnp.where(keep, up_s[:, at].astype(jnp.float32), 0.0).astype(jnp.bfloat16)

    pl.semaphore_wait(barrier, len(near))

    def tell(n):
        for to in beside_x if n == 0 else beside_y:
            pl.semaphore_signal(news.at[n], inc=1, device_id=(to, col), device_id_type=MESH)

    def hear(n):
        pl.semaphore_wait(news.at[n], 2)
        if n < NY // 2:
            tell(n + 1)

    tell(0)

    def send(ref, send_sem, recv_sem, to):
        return pltpu.make_async_remote_copy(
            src_ref=ref, dst_ref=ref, send_sem=send_sem, recv_sem=recv_sem, device_id=to, device_id_type=MESH
        )

    halves = pl.ds(0, ROWS // 2), pl.ds(ROWS // 2, ROWS // 2)

    def up(q, s, far, slot):
        n = q * 8 + s * 2 + far
        return send(dz.at[q, slot, halves[1 - far]], up_send.at[n], up_recv.at[n], (dp, above))

    def dn(q, s, far, slot):
        n = q * 8 + s * 2 + far
        return send(dz.at[q, slot, halves[far]], dn_send.at[n], dn_recv.at[n], (dp, below))

    def sib(q, i, slot):
        return send(dz.at[q, slot], sib_send.at[q, i], sib_recv.at[q, i], (dp, sibling))

    for far in (1, 0):
        for q in range(C):
            up(q, 0, far, col).start()
            dn(q, 0, far, col).start()
    for q in range(C):
        sib(q, 0, col).start()

    def serve(q, s, far):
        from_below = (z + NZ - 1 - s) % NZ * 2 + core
        from_above = (z + 1 + s) % NZ * 2 + core
        onward = s < 2 + far
        up(q, s, far, from_below).wait_recv()
        if onward:
            up(q, s + 1, far, from_below).start()
        dn(q, s, far, from_above).wait_recv()
        if onward:
            dn(q, s + 1, far, from_above).start()
        if s == 3:
            sib(q, 7, from_below).start()
        elif not far:
            sib(q, s + 1, from_below).start()
            sib(q, s + 4, from_above).start()

    def add(dz_, i, chunks=range(C)):
        at = (z + NZ + dz_) % NZ
        rows = lhs[:, pl.ds(pl.multiple_of(at * 2 * ROWS, 2 * ROWS), 2 * ROWS)]
        for q in chunks:
            sib(q, i, at * 2 + 1 - core).wait_recv()
            new = jnp.dot(rows, dz[q, pl.ds(at * 2, 2)].reshape(2 * ROWS, W), preferred_element_type=jnp.float32)
            here = slice(q * W, (q + 1) * W)
            acc[:, here] = new if dz_ == 0 else acc[:, here] + new

    loads[2].wait()
    loads[3].wait()
    encode(nbr_s, deg_s, hi_s, lo_s)
    loads[4].wait()

    def step(i, _):
        aggregate_block(i, src_s, hi_s, lo_s, tal, agg_s)
        for at, turn in ((2, (0, 0, 1)), (3, (1, 0, 1)), (4, (0, 0, 0)), (5, (1, 0, 0)), (6, (0, 1, 1)), (7, (1, 1, 1))):
            pl.when(i == at)(lambda turn=turn: serve(*turn))
        for at, n in ((3, 0), (5, 1), (7, 2)):
            pl.when(i == at)(lambda n=n: hear(n))
        return 0

    lax.fori_loop(0, 8, step, 0)

    lhs[0:F] = src_s[:, 0:T]
    for j in range(8):
        at = slice(j * 256, (j + 1) * 256)
        total = agg_s[pl.ds(j, 256, stride=8), :].T
        lhs[F : 2 * F, at] = (total[0:F] / jnp.maximum(deg_s[:, at], 1).astype(jnp.float32)).astype(jnp.bfloat16)
    lhs[2 * F : 2 * F + 16] = jnp.ones((16, T), jnp.bfloat16)

    hear(3)
    add(0, 0)
    serve(0, 1, 0)
    serve(1, 1, 0)
    add(-1, 1)
    add(1, 4)
    serve(0, 2, 1)
    serve(1, 2, 1)
    add(-2, 2)
    add(2, 5)
    serve(0, 2, 0)
    serve(1, 2, 0)
    add(-3, 3)
    add(3, 6)

    for q in range(C):
        serve(q, 3, 1)
        add(4, 7, (q,))
        for b in range(q * 8 // C, (q + 1) * 8 // C):
            at = slice(b * 128, (b + 1) * 128)
            for a in range(4):
                part[a * 8 + b, 0:16] = acc[a * 24 : a * 24 + 16, at].astype(jnp.bfloat16)
    bias = jnp.concatenate([acc[2 * F : 2 * F + 1, b * 128 : (b + 1) * 128] for b in range(8)], axis=0)

    def finish_part():
        for b in range(8):
            at = slice(b * 128, (b + 1) * 128)
            for a in range(4):
                rows = acc[a * 24 + 16 : a * 24 + 24, at]
                part[a * 8 + b, 16:32] = jnp.concatenate([rows, bias], axis=0).astype(jnp.bfloat16)

    hear(4)

    def scatter(n):
        half = pl.ds(n * 16, 16)
        for p in PEERS:
            pltpu.make_async_remote_copy(
                src_ref=part.at[peer(*p), half], dst_ref=rs.at[n, dp], send_sem=rs_send.at[n], recv_sem=rs_recv.at[n],
                device_id=(peer(*p), col), device_id_type=MESH,
            ).start()
        rs[n, dp] = part[dp, n * 16 : n * 16 + 16]

    scale = jnp.float32(1.0) / jnp.sqrt(jnp.float32(T * NDP))

    def tile(owner, n):
        rows = pl.ds(pl.multiple_of(owner // 8 * 24 + n * 16, 8), 16 - 8 * n)
        return grad_ref.at[rows, pl.ds(pl.multiple_of(owner % 8 * 128, 128), 128)]

    def along_x(ref, owner, n):
        for dx in (2, 1, 3):
            pltpu.make_async_remote_copy(
                src_ref=ref, dst_ref=tile(owner, n), send_sem=x_send.at[n], recv_sem=x_recv.at[n],
                device_id=(peer(0, dx), col), device_id_type=MESH,
            ).start()
        pltpu.make_async_copy(ref, tile(owner, n), own_sem.at[n]).start()

    def along_y(n, dy):
        return pltpu.make_async_remote_copy(
            src_ref=mine.at[n, pl.ds(0, 16 - 8 * n)], dst_ref=stage.at[n, dy, pl.ds(0, 16 - 8 * n)],
            send_sem=y_send.at[n], recv_sem=y_recv.at[n * NY + dy], device_id=(peer(dy, 0), col), device_id_type=MESH,
        )

    def spread(n):
        every = rs.at[n, pl.ds(0, NP)]
        pltpu.make_async_copy(every, every, rs_recv.at[n]).wait()
        total = rs[n, 0].astype(jnp.float32)
        for d in range(1, NDP):
            total += rs[n, d].astype(jnp.float32)
        mine[n] = total * scale
        if n == 1:
            for p in PEERS:
                pltpu.make_async_remote_copy(
                    src_ref=mine.at[n, pl.ds(0, 8)], dst_ref=tile(dp, n), send_sem=x_send.at[n], recv_sem=x_recv.at[n],
                    device_id=(peer(*p), col), device_id_type=MESH,
                ).start()
            pltpu.make_async_copy(mine.at[n, pl.ds(0, 8)], tile(dp, n), own_sem.at[n]).start()
            pltpu.make_async_copy(mine.at[n, pl.ds(8, 8)], bias_ref, bias_sem).start()
            return
        for dy in (4, 3, 5, 2, 6, 1, 7):
            along_y(n, dy).start()
        along_x(mine.at[n, pl.ds(0, 16)], dp, n)

    def pass_on(n):
        for dy in (1, 7, 2, 6, 3, 5, 4):
            along_y(n, dy).wait_recv()
            along_x(stage.at[n, dy, pl.ds(0, 16 - 8 * n)], peer(NY - dy, 0), n)

    scatter(0)
    finish_part()
    scatter(1)
    spread(0)
    spread(1)
    pass_on(0)

    for q in range(C):
        for s in range(4):
            for far in (1, 0) if s < 3 else (1,):
                up(q, s, far, col).wait_send()
                dn(q, s, far, col).wait_send()
        for i in range(8):
            sib(q, i, col).wait_send()
    def as_many(tiles, n):
        return agg_s.at[pl.ds(0, tiles * (16 - 8 * n))]

    pltpu.make_async_copy(mine.at[1, pl.ds(8, 8)], bias_ref, bias_sem).wait()
    for n in range(2):
        sent = rs.at[n, pl.ds(0, NP)]
        pltpu.make_async_copy(sent, sent, rs_send.at[n]).wait()
        relayed = ((y_send, NY - 1), (own_sem, NY), (x_send, NY * (NX - 1)), (x_recv, NY * (NX - 1)))
        direct = ((own_sem, 1), (x_send, NP), (x_recv, NP))
        for sem, tiles in direct if n else relayed:
            pltpu.make_async_copy(as_many(tiles, n), as_many(tiles, n), sem.at[n]).wait()


def place(grad_ref, bias_ref, self_ref, neigh_ref, out_ref):
    self_ref[...] = grad_ref[0:F]
    neigh_ref[...] = grad_ref[F : 2 * F]
    out_ref[...] = bias_ref[...]


def per_device(source_feats, neighbours, degree, counts, upstream, preact):
    any_, vmem = pl.BlockSpec(memory_space=pl.ANY), pl.BlockSpec(memory_space=pltpu.VMEM)
    dma = pltpu.SemaphoreType.DMA
    f32, bf16, i32 = jnp.float32, jnp.bfloat16, jnp.int32
    grad, bias = pl.pallas_call(
        kernel,
        out_shape=(jax.ShapeDtypeStruct((2 * F, H), f32), jax.ShapeDtypeStruct((8, 128), f32)),
        in_specs=[any_, any_, any_, pl.BlockSpec(memory_space=pltpu.SMEM), any_, any_],
        out_specs=(any_, any_),
        scratch_shapes=[
            pltpu.VMEM((F, 4096), bf16),
            pltpu.VMEM((25, T), i32),
            pltpu.VMEM((1, T), i32),
            pltpu.VMEM((ROWS, H), bf16),
            pltpu.VMEM((ROWS, H), bf16),
            pltpu.VMEM((256, 256), f32),
            pltpu.VMEM((256, 256), f32),
            pltpu.VMEM((16, 256, 256), bf16),
            pltpu.VMEM((T + 8, 128), f32),
            pltpu.VMEM((2 * F + 16, T), bf16),
            pltpu.VMEM((C, NCOL, ROWS, W), bf16),
            pltpu.VMEM((2 * F + 16, H), f32),
            pltpu.VMEM((NDP, 32, 128), bf16),
            pltpu.VMEM((2, NDP, 16, 128), bf16),
            pltpu.VMEM((2, 16, 128), f32),
            pltpu.VMEM((2, NY, 16, 128), f32),
            dma((5,)),
            dma((C * 8,)), dma((C * 8,)), dma((C * 8,)), dma((C * 8,)), dma((C, 8)), dma((C, 8)),
            dma((2,)), dma((2,)), dma((2,)), dma((2 * NY,)), dma((2,)), dma((2,)), dma((2,)), dma(()), pltpu.SemaphoreType.REGULAR((NY // 2 + 1,)),
        ],
        compiler_params=pltpu.CompilerParams(collective_id=0, has_side_effects=True, vmem_limit_bytes=60 << 20),
        name="sage_grads",
    )(source_feats, neighbours.T, degree.reshape(1, T), counts, upstream, preact)
    own, neigh, bias = pl.pallas_call(
        place,
        out_shape=(jax.ShapeDtypeStruct((F, H), f32), jax.ShapeDtypeStruct((F, H), f32), jax.ShapeDtypeStruct((8, 128), f32)),
        in_specs=[vmem, vmem],
        out_specs=(vmem, vmem, vmem),
        compiler_params=pltpu.CompilerParams(vmem_limit_bytes=60 << 20),
        name="place",
    )(grad, bias)
    return own, neigh, bias.reshape(H)


def solution(mesh):
    placed = (P("col", "dp"), P("dp", None), P("dp"), P("dp"), P(("dp", "col"), None), P(("dp", "col"), None))
    return jax.shard_map(
        per_device,
        mesh=mesh,
        in_specs=placed,
        out_specs=(P("col", None), P("col", None), P()),
        check_vma=False,
    )
```
